32 devices in a mesh: groups: 2 (over x), expert: 16 (over z, y, core).
Axes of the slice: x: 2, y: 2, z: 4, core: 2. Of those that a mesh axis runs over, the one named last changes fastest.
Arguments:
- hidden_states: bfloat16 [2, 512, 4096], P(None, ('groups', 'expert')), parts along dimension 1, may hold values from -6 to 6
- expert_ids: int32 [2, 512, 8], P(None, ('groups', 'expert')), parts along dimension 1, may hold values from 0 to 15, all different within a row; in each aligned block of 16 rows (0 to 15, 16 to 31, ..., all dimensions but the last counted through in order) at most 16 rows name the same one
- router_probs: float32 [2, 512, 8], P(None, ('groups', 'expert')), parts along dimension 1, may hold values from 0.05 to 1
- swap_flags: int32 [16], replicated, may hold values from 0 to 1, as said below
- w_gate: bfloat16 [16, 4096, 768], P('expert'), may hold values from -0.09375 to 0.09375
- w_up: bfloat16 [16, 4096, 768], P('expert'), may hold values from -0.09375 to 0.09375
- w_down: bfloat16 [16, 768, 4096], P('expert'), may hold values from -0.21875 to 0.21875
Outputs:
- mixed: bfloat16 [2, 512, 4096], P(None, ('groups', 'expert')), parts along dimension 1
The draws below stay inside these ranges and needn't reach their ends.
There are 2 independent parts, one for each index of `groups`. The reference program is written for one: setup_inputs(seed, part) draws one part's arguments, and reference() takes and returns one part's arrays. A program takes and returns all parts, laid end to end along the dimension named above; an argument that names none is the same for every part. Nothing has to cross between parts.
Inputs may be any that keep to these rules, and one draw needn't show every extreme that they name: `expert_ids`: within one step, the 16 rows of one device (aligned blocks of 16 rows) name any one slot at most 16 times, a bound that some block reaches; the 8 ids of a row differ. swap_flags[e] equals swap_flags[e XOR 1] for every slot e.
All inputs are finite; a program needn't handle non-finite values.
Results may differ from the reference program's by a relative error of at most 0.0058.
Values may be sent and summed in bfloat16 or wider, within the bound.
No kernel may reach another device: no remote copies, remote signals or barrier semaphores. Data moves between devices by JAX's collectives and lax.ppermute only.
A program may use at most 128 MiB of HBM per device.

```python
import math
import jax
import jax.numpy as jnp
import numpy as np
from jax import lax

D = 4096
FW = 768
TOPK = 8
STEPS = 2
TOK_DEV = 16
EXPERTS = 16
TOKENS = 256
CAP = 16
N_EXPERT = 16


def draw_swap_flags(key, part):
    pair_flags = jax.random.randint(jax.random.fold_in(key, 7), (EXPERTS // 2,), 0, 2).astype(jnp.int32)
    return jnp.repeat(pair_flags, 2).astype(jnp.int32)


def block_scale(own_key, shape, shards, low, high):
    level, own = 1.0, jax.random.fold_in(own_key, 6)
    for dim, parts in shards:
        steps = jnp.exp(jax.random.uniform(jax.random.fold_in(own, dim), (parts,), jnp.float32, low / len(shards), high / len(shards)))
        level = level * jnp.repeat(steps, shape[dim] // parts).reshape([-1 if axis == dim else 1 for axis in range(len(shape))])
    return level


def routed_block(own_key, own, number, rows, number_of, top, bound, skew):
    sequence = jax.random.permutation(own_key, number_of)
    crowded, usual = load_shares(number_of, rows * top, bound, skew, True), load_shares(number_of, rows * top, bound, skew, False)
    places = jnp.arange(number_of)

    def named(tallies, offset_by):
        used = int((tallies > 0).sum())
        fixed = max(1, used // 4)
        shifted = fixed + (places - fixed + offset_by * (used - fixed)) % max(1, number_of - fixed)
        return jnp.zeros((number_of,), jnp.int32).at[sequence[jnp.where(places < fixed, places, shifted)]].set(jnp.asarray(tallies, jnp.int32))

    tallies = jnp.where(number % 4 == 0, named(crowded, number // 4), named(usual, number - number // 4 - 1))
    mixed = jax.random.permutation(jax.random.fold_in(own, 3), number_of)
    source_of, taker = mixed[0:number_of // 2 * 2:2], mixed[1:number_of // 2 * 2:2]
    margin = jnp.minimum(tallies[source_of] - 1, bound - tallies[taker]) // 2
    margin = jnp.where((source_of == sequence[0]) | (taker == sequence[0]) | (tallies[taker] == 0), 0, jnp.maximum(margin, 0))
    shifted = jax.random.randint(jax.random.fold_in(own, 4), (number_of // 2,), 0, 1 << 20) % (margin + 1)
    tallies = tallies.at[source_of].add(-shifted).at[taker].add(shifted)
    members = jnp.searchsorted(jnp.cumsum(tallies), jnp.arange(rows * top), side="right").astype(jnp.int32)
    listing = members.reshape(top, rows).T
    listing = listing[jax.random.permutation(jax.random.fold_in(own, 1), rows)]
    offset_by = jax.random.randint(jax.random.fold_in(own, 2), (rows, 1), 0, top)
    return jnp.take_along_axis(listing, (jnp.arange(top)[None, :] + offset_by) % top, axis=1)


def load_shares(number_of, total, bound, slope, full):
    portions = [(1 << 20) // math.isqrt(grade ** slope) + 1 for grade in range(1, number_of + 1)]
    largest = bound if full else min(bound, max(-(-total // number_of), total * portions[0] // sum(portions)))
    least = 1 if total - largest >= number_of - 1 else 0
    holding, spare = [largest] + [least] * (number_of - 1), total - largest - least * (number_of - 1)
    while spare > 0:
        movable = [i for i in range(1, number_of) if holding[i] < largest] or [i for i in range(1, number_of) if holding[i] < bound]
        whole, budget = sum([portions[i] for i in movable]), spare
        for i in movable:
            more = min(bound - holding[i], max(1, budget * portions[i] // whole), spare)
            holding[i] = holding[i] + more
            spare = spare - more
    return np.array(holding)


def scatter_about(rng, extent, scale, bound, pieces=(), kind=jnp.bfloat16):
    entries = scale * jax.random.normal(rng, extent, jnp.float32)
    if pieces:
        entries = entries * block_scale(rng, extent, pieces, -0.22, 0.18)
    return jnp.clip(entries, -bound, bound).astype(kind)


def setup_inputs(seed: int = 0, part: int = 0) -> dict:
    key_list = jax.random.split(jax.random.key(seed), 8)
    part_keys = jax.random.split(jax.random.fold_in(key_list[7], part), 8)
    hidden_states = scatter_about(part_keys[0], (STEPS, TOKENS, D), 1.0, 6.0, ((1, 16),))
    expert_ids_keys = jax.random.split(jax.random.fold_in(part_keys[1], 1), STEPS * TOKENS // TOK_DEV)
    expert_ids_turns = jax.random.permutation(jax.random.fold_in(part_keys[1], 3), STEPS * TOKENS // TOK_DEV)
    expert_ids = jax.vmap(lambda own, number: routed_block(jax.random.fold_in(part_keys[1], 2), own, number, TOK_DEV, EXPERTS, TOPK, CAP, 2))(expert_ids_keys, expert_ids_turns).reshape((STEPS, TOKENS, TOPK))
    router_probs = jnp.clip(jnp.exp(math.log(1.0) - 2.9957323 * jax.random.uniform(part_keys[2], (STEPS, TOKENS, TOPK), jnp.float32) ** block_scale(part_keys[2], (STEPS, TOKENS, TOPK), ((1, 16),), -0.2, 0.2)), 0.05, 1.0)
    swap_flags = draw_swap_flags(jax.random.fold_in(key_list[7], 71), part)
    w_gate = scatter_about(key_list[4], (EXPERTS, D, FW), D ** -0.5, 0.09375, ((0, 16),))
    w_up = scatter_about(key_list[5], (EXPERTS, D, FW), D ** -0.5, 0.09375, ((0, 16),))
    w_down = scatter_about(key_list[6], (EXPERTS, FW, D), FW ** -0.5, 0.21875, ((0, 16),))
    return {"hidden_states": hidden_states, "expert_ids": expert_ids, "router_probs": router_probs, "swap_flags": swap_flags, "w_gate": w_gate, "w_up": w_up, "w_down": w_down}


def expert_mlp(rows, gate_matrix, up_matrix, down_matrix):
    gate = jnp.dot(rows, gate_matrix, preferred_element_type=jnp.float32)
    up_part = jnp.dot(rows, up_matrix, preferred_element_type=jnp.float32)
    hidden = (jax.nn.silu(gate) * up_part).astype(jnp.bfloat16)
    return jnp.dot(hidden, down_matrix, preferred_element_type=jnp.float32).astype(jnp.bfloat16)


def apply_expert(operands):
    return expert_mlp(operands[0], operands[1], operands[2], operands[3])


def reference(hidden_states, expert_ids, router_probs, swap_flags, w_gate, w_up, w_down):
    outputs = []
    slots_iota = jnp.arange(EXPERTS, dtype=jnp.int32)
    partner = jnp.bitwise_xor(slots_iota, 1).astype(jnp.int32)
    for step_index in range(STEPS):
        if step_index == 0:
            held = slots_iota
        else:
            held = jnp.where(swap_flags == 1, partner, slots_iota).astype(jnp.int32)
        states = hidden_states[step_index]
        routed = expert_ids[step_index]
        weights_raw = router_probs[step_index]
        shares = weights_raw / jnp.sum(weights_raw, axis=-1, keepdims=True)
        blocks = routed.reshape(N_EXPERT, TOK_DEV * TOPK)
        onehot = (blocks[:, :, None] == slots_iota[None, None, :]).astype(jnp.int32)
        before = (jnp.cumsum(onehot, axis=1).astype(jnp.int32) - onehot) * onehot
        slot_rank = jnp.sum(before, axis=2).astype(jnp.int32)
        source = jnp.arange(N_EXPERT, dtype=jnp.int32)[:, None]
        target = (blocks * (N_EXPERT * CAP) + source * CAP + slot_rank).reshape(-1).astype(jnp.int32)
        token_row = (source * TOK_DEV + jnp.arange(TOK_DEV * TOPK, dtype=jnp.int32)[None, :] // TOPK).reshape(-1).astype(jnp.int32)
        row_table = jnp.full((EXPERTS * N_EXPERT * CAP,), TOKENS, jnp.int32).at[target].set(token_row)
        padded = jnp.concatenate([states, jnp.zeros((1, D), jnp.bfloat16)], axis=0)
        gathered = padded[row_table].reshape(EXPERTS, N_EXPERT * CAP, D)
        results = lax.map(apply_expert, (gathered, w_gate[held], w_up[held], w_down[held]))
        picked = results.reshape(-1, D)[target].reshape(TOKENS, TOPK, D).astype(jnp.float32)
        outputs.append(jnp.sum(shares[:, :, None] * picked, axis=1).astype(jnp.bfloat16))
    return jnp.stack(outputs)
```

```python
import functools

import jax
import jax.numpy as jnp
from jax import lax
from jax.experimental import pallas as pl
from jax.experimental.pallas import tpu as pltpu
from jax.sharding import PartitionSpec as P

LANES = 128
MIB = 1 << 20


def in_vmem():
    return pl.BlockSpec(memory_space=pltpu.VMEM)


def message_kernel(states_ref, ids_ref, probs_ref, *message_refs):
    width = states_ref.shape[2]
    tail = message_refs[0].shape[1] - width
    half = tail // 2
    for step, message_ref in enumerate(message_refs):
        probs = probs_ref[step]
        share = probs / jnp.sum(probs, axis=1, keepdims=True)
        ids = ids_ref[step]
        lane = lax.broadcasted_iota(jnp.int32, (ids.shape[0], tail), 1)
        slot = lane % half
        dense = jnp.zeros((ids.shape[0], tail), jnp.float32)
        for k in range(ids.shape[1]):
            dense += jnp.where(ids[:, k : k + 1] == slot, share[:, k : k + 1], 0.0)
        high = dense.astype(jnp.bfloat16).astype(jnp.float32)
        message_ref[:, :width] = states_ref[step]
        message_ref[:, width:] = jnp.where(lane < half, high, dense - high).astype(jnp.bfloat16)


def make_messages(states, ids, probs, tail):
    steps, tokens, width = states.shape
    return pl.pallas_call(
        message_kernel,
        out_shape=[jax.ShapeDtypeStruct((tokens, width + tail), jnp.bfloat16)] * steps,
        in_specs=[in_vmem()] * 3,
        out_specs=[in_vmem()] * steps,
        name="messages",
    )(states, ids, probs)


def expert_kernel(
    slot_ref, first, second, third, fourth, gate_ref, up_ref, down_ref, own_ref, other_ref, rows, hidden
):
    width, units = gate_ref.shape
    tail = first.shape[1] - width
    count = first.shape[0]
    slot = slot_ref[0]
    for part, source in enumerate((first, second, third, fourth)):
        rows[part * count : (part + 1) * count] = source[...]
    total = rows.shape[0]
    lane = lax.broadcasted_iota(jnp.int32, (total, tail), 1)
    terms = rows[:, width:].astype(jnp.float32)
    weight = jnp.sum(jnp.where(lane % (tail // 2) == slot, terms, 0.0), axis=1, keepdims=True)
    step = 256
    for at in range(0, units, step):
        gate = jnp.dot(rows[:, :width], gate_ref[:, at : at + step], preferred_element_type=jnp.float32)
        up = jnp.dot(rows[:, :width], up_ref[:, at : at + step], preferred_element_type=jnp.float32)
        value = gate / (1.0 + jnp.exp(-gate)) * up
        hidden[:, at : at + step] = (value * weight).astype(jnp.bfloat16)

    def columns(index, _):
        at = pl.ds(pl.multiple_of(index * 512, 512), 512)
        out = jnp.dot(hidden[...], down_ref[:, at], preferred_element_type=jnp.float32)
        out = out.astype(jnp.bfloat16)
        own_ref[:, at] = out[: total // 2]
        other_ref[:, at] = out[total // 2 :]
        return 0

    lax.fori_loop(0, width // 512, columns, 0)


def run_expert(slot, parts, gate, up, down):
    count = parts[0].shape[0]
    width, units = gate.shape
    gate, up, down = (pltpu.with_memory_space_constraint(w, pltpu.VMEM) for w in (gate, up, down))
    return pl.pallas_call(
        expert_kernel,
        out_shape=[jax.ShapeDtypeStruct((2 * count, width), jnp.bfloat16)] * 2,
        in_specs=[pl.BlockSpec(memory_space=pltpu.SMEM)] + [in_vmem()] * 7,
        out_specs=[in_vmem()] * 2,
        scratch_shapes=[
            pltpu.VMEM((4 * count, parts[0].shape[1]), jnp.bfloat16),
            pltpu.VMEM((4 * count, units), jnp.bfloat16),
        ],
        compiler_params=pltpu.CompilerParams(vmem_limit_bytes=28 * MIB),
        cost_estimate=pl.CostEstimate(
            flops=4 * count * width * units * 6, bytes_accessed=16 * count * width, transcendentals=0
        ),
        name="expert",
    )(slot, *parts, gate, up, down)


def on_device(states, ids, probs, flags, w_gate, w_up, w_down):
    devices = lax.axis_size("expert")
    owner = lax.axis_index("expert")
    lines = devices // 4
    steps, tokens, width = states.shape

    def index(far, near, core):
        return far * 4 + near * 2 + core

    every = [(z, y, c) for z in range(lines) for y in range(2) for c in range(2)]

    def swap_core(x):
        return lax.ppermute(x, "expert", [(index(z, y, c), index(z, y, 1 - c)) for z, y, c in every])

    def swap_near(x):
        return lax.ppermute(x, "expert", [(index(z, y, c), index(z, 1 - y, c)) for z, y, c in every])

    def shift_far(x, by):
        return lax.ppermute(x, "expert", [(index(z, y, c), index((z + by) % lines, y, c)) for z, y, c in every])

    tail = 2 * devices
    tail = -(-tail // LANES) * LANES
    messages = list(make_messages(states, ids, probs, tail))
    gate, up, down = w_gate[0], w_up[0], w_down[0]
    flag = lax.dynamic_index_in_dim(flags, owner, keepdims=True)
    outputs = []
    gathered = []
    for step in range(steps):
        message = messages[step]
        if step:
            message, _ = lax.optimization_barrier((message, gathered[step - 1][0]))
        line = jnp.concatenate([message] + [shift_far(message, by) for by in range(1, lines)], axis=0)
        near = swap_near(line)
        gathered.append((line, near, swap_core(line), swap_core(near)))
    for step in range(steps):
        slot = jnp.bitwise_xor(owner, flag) if step else jnp.full((1,), 0, jnp.int32) + owner
        own, other = run_expert(slot.astype(jnp.int32), gathered[step], gate, up, down)
        other = swap_core(other)
        half = own.shape[0] // 2
        both = own.astype(jnp.float32) + other.astype(jnp.float32)
        near = swap_near(both[half:].astype(jnp.bfloat16))
        line = both[:half] + near.astype(jnp.float32)
        line = line.reshape(lines, tokens, width)
        mixed = line[0]
        for by in range(1, lines):
            mixed += shift_far(line[by].astype(jnp.bfloat16), lines - by).astype(jnp.float32)
        outputs.append(mixed.astype(jnp.bfloat16))
    return jnp.stack(outputs)


def solution(mesh):
    rows = P(None, ("groups", "expert"), None)
    weights = P("expert", None, None)
    return jax.shard_map(
        on_device,
        mesh=mesh,
        in_specs=(rows, rows, rows, P(), weights, weights, weights),
        out_specs=rows,
        check_vma=False,
    )
```

```python
import functools

import jax
import jax.numpy as jnp
from jax import lax
from jax.experimental import pallas as pl
from jax.experimental.pallas import tpu as pltpu
from jax.sharding import PartitionSpec as P

LANES = 128
MIB = 1 << 20


def in_vmem():
    return pl.BlockSpec(memory_space=pltpu.VMEM)


def message_kernel(states_ref, ids_ref, probs_ref, message_ref):
    tokens, width = states_ref.shape
    tail = message_ref.shape[1] - width
    half = tail // 2
    probs = probs_ref[...]
    share = probs / jnp.sum(probs, axis=0, keepdims=True)
    ids = ids_ref[...]
    place = lax.broadcasted_iota(jnp.int32, (tail, tokens), 0)
    dense = jnp.zeros((tail, tokens), jnp.float32)
    for k in range(ids.shape[0]):
        dense += jnp.where(ids[k : k + 1] == place % half, share[k : k + 1], 0.0)
    high = dense.astype(jnp.bfloat16).astype(jnp.float32)
    terms = jnp.where(place < half, high, dense - high).astype(jnp.bfloat16)
    row = lax.broadcasted_iota(jnp.int32, (tokens, tokens), 0)
    column = lax.broadcasted_iota(jnp.int32, (tokens, tokens), 1)
    one = jnp.where(row == column, 1.0, 0.0).astype(jnp.bfloat16)
    upright = lax.dot_general(one, terms, (((1,), (1,)), ((), ())), preferred_element_type=jnp.float32)
    message_ref[:, :width] = states_ref[...]
    message_ref[:, width:] = upright.astype(jnp.bfloat16)


def make_message(states, ids, probs, step, tail):
    _, tokens, width = states.shape

    def of_step(x):
        return pl.BlockSpec((None,) + x.shape[1:], lambda i: (step, 0, 0))

    return pl.pallas_call(
        message_kernel,
        grid=(1,),
        out_shape=jax.ShapeDtypeStruct((tokens, width + tail), jnp.bfloat16),
        in_specs=[of_step(states), of_step(ids), of_step(probs)],
        out_specs=pl.BlockSpec((tokens, width + tail), lambda i: (0, 0)),
        compiler_params=pltpu.CompilerParams(vmem_limit_bytes=4 * MIB),
        name="message",
    )(states, ids, probs)


def load_kernel(*refs):
    count = len(refs) // 3
    copies = [
        pltpu.make_async_copy(refs[i], refs[count + i], refs[2 * count + i]) for i in range(count)
    ]
    for copy in copies:
        copy.start()
    for copy in copies:
        copy.wait()


def load_weights(*arrays):
    arrays = [pltpu.with_memory_space_constraint(x, pltpu.HBM) for x in arrays]
    return pl.pallas_call(
        load_kernel,
        out_shape=[pltpu.VMEM(x.shape, x.dtype) for x in arrays],
        in_specs=[pl.BlockSpec(memory_space=pltpu.HBM)] * len(arrays),
        out_specs=[in_vmem()] * len(arrays),
        scratch_shapes=[pltpu.SemaphoreType.DMA(())] * len(arrays),
        cost_estimate=pl.CostEstimate(
            flops=0, bytes_accessed=sum(2 * x.size for x in arrays), transcendentals=0
        ),
        compiler_params=pltpu.CompilerParams(vmem_limit_bytes=4 * MIB),
        name="load_weights",
    )(*arrays)


def expert_kernel(
    swapped, flags_ref, first, second, third, fourth, gate_ref, up_ref, down_ref, own_ref, near_ref, other_ref, rows, hidden
):
    width, units = gate_ref.shape
    tail = first.shape[1] - width
    count = first.shape[0]
    owner = lax.axis_index("expert")
    slot = jnp.bitwise_xor(owner, flags_ref[owner]) if swapped else owner
    for part, source in enumerate((first, second, third, fourth)):
        rows[part * count : (part + 1) * count] = source[...]
    total = rows.shape[0]
    lane = lax.broadcasted_iota(jnp.int32, (total, tail), 1)
    terms = rows[:, width:].astype(jnp.float32)
    weight = jnp.sum(jnp.where(lane % (tail // 2) == slot, terms, 0.0), axis=1, keepdims=True)
    step = 256
    for at in range(0, units, step):
        gate = jnp.dot(rows[:, :width], gate_ref[:, at : at + step], preferred_element_type=jnp.float32)
        up = jnp.dot(rows[:, :width], up_ref[:, at : at + step], preferred_element_type=jnp.float32)
        value = gate / (1.0 + jnp.exp(-gate)) * up
        hidden[:, at : at + step] = (value * weight).astype(jnp.bfloat16)

    def columns(index, _):
        at = pl.ds(pl.multiple_of(index * 512, 512), 512)
        out = jnp.dot(hidden[...], down_ref[:, at], preferred_element_type=jnp.float32)
        out = out.astype(jnp.bfloat16)
        own_ref[:, at] = out[:count]
        near_ref[:, at] = out[count : 2 * count]
        other_ref[:, at] = out[2 * count :]
        return 0

    lax.fori_loop(0, width // 512, columns, 0)


def run_expert(swapped, flags, parts, gate, up, down):
    count = parts[0].shape[0]
    width, units = gate.shape
    gate, up, down = (pltpu.with_memory_space_constraint(w, pltpu.VMEM) for w in (gate, up, down))
    return pl.pallas_call(
        functools.partial(expert_kernel, swapped),
        out_shape=[jax.ShapeDtypeStruct((k * count, width), jnp.bfloat16) for k in (1, 1, 2)],
        in_specs=[pl.BlockSpec(memory_space=pltpu.SMEM)] + [in_vmem()] * 7,
        out_specs=[in_vmem()] * 3,
        scratch_shapes=[
            pltpu.VMEM((4 * count, parts[0].shape[1]), jnp.bfloat16),
            pltpu.VMEM((4 * count, units), jnp.bfloat16),
        ],
        compiler_params=pltpu.CompilerParams(vmem_limit_bytes=16 * MIB),
        cost_estimate=pl.CostEstimate(
            flops=4 * count * width * units * 6, bytes_accessed=16 * count * width, transcendentals=0
        ),
        name="expert",
    )(flags, *parts, gate, up, down)


def on_device(states, ids, probs, flags, w_gate, w_up, w_down):
    devices = lax.axis_size("expert")
    lines = devices // 4
    steps, tokens, width = states.shape

    def index(far, near, core):
        return far * 4 + near * 2 + core

    every = [(z, y, c) for z in range(lines) for y in range(2) for c in range(2)]

    def swap_core(x):
        return lax.ppermute(x, "expert", [(index(z, y, c), index(z, y, 1 - c)) for z, y, c in every])

    def swap_near(x):
        return lax.ppermute(x, "expert", [(index(z, y, c), index(z, 1 - y, c)) for z, y, c in every])

    def shift_far(x, by):
        return lax.ppermute(x, "expert", [(index(z, y, c), index((z + by) % lines, y, c)) for z, y, c in every])

    tail = 2 * devices
    tail = -(-tail // LANES) * LANES
    ids, probs = jnp.swapaxes(ids, 1, 2), jnp.swapaxes(probs, 1, 2)
    weights = load_weights(w_gate[0], w_up[0], w_down[0])
    messages = [make_message(states, ids, probs, step, tail) for step in range(steps)]
    gathered = []
    for step in range(steps):
        message = messages[step]
        if step:
            message, _ = lax.optimization_barrier((message, gathered[step - 1][2]))
        blocks = [message] + [shift_far(message, by) for by in range(1, lines)]
        if not step:
            blocks, weights, messages[1:] = lax.optimization_barrier((blocks, weights, messages[1:]))
        line = jnp.concatenate(blocks, axis=0)
        near = swap_near(line)
        gathered.append((line, near, swap_core(line), swap_core(near)))
    outputs = []
    other = None
    for step in range(steps):
        parts = gathered[step]
        if step:
            parts, _ = lax.optimization_barrier((parts, other))
        own, peer, other = run_expert(step > 0, flags, parts, *weights)
        other = swap_core(other)
        half = own.shape[0]
        peer = peer.astype(jnp.float32) + other[half:].astype(jnp.float32)
        near = swap_near(peer.astype(jnp.bfloat16))
        line = own.astype(jnp.float32) + other[:half].astype(jnp.float32) + near.astype(jnp.float32)
        line = line.reshape(lines, tokens, width)
        mixed = line[0]
        for by in range(1, lines):
            mixed += shift_far(line[by].astype(jnp.bfloat16), lines - by).astype(jnp.float32)
        outputs.append(mixed.astype(jnp.bfloat16))
    return jnp.stack(outputs)


def solution(mesh):
    rows = P(None, ("groups", "expert"), None)
    weights = P("expert", None, None)
    return jax.shard_map(
        on_device,
        mesh=mesh,
        in_specs=(rows, rows, rows, P(), weights, weights, weights),
        out_specs=rows,
        check_vma=False,
    )
```

```python
import functools

import jax
import jax.numpy as jnp
from jax import lax
from jax.experimental import pallas as pl
from jax.experimental.pallas import tpu as pltpu
from jax.sharding import PartitionSpec as P

LANES = 128
MIB = 1 << 20


def in_vmem():
    return pl.BlockSpec(memory_space=pltpu.VMEM)


def message_kernel(states_ref, ids_ref, probs_ref, message_ref):
    tokens, width = states_ref.shape
    tail = message_ref.shape[1] - width
    half = tail // 2
    probs = probs_ref[...]
    share = probs / jnp.sum(probs, axis=0, keepdims=True)
    ids = ids_ref[...]
    place = lax.broadcasted_iota(jnp.int32, (tail, tokens), 0)
    dense = jnp.zeros((tail, tokens), jnp.float32)
    for k in range(ids.shape[0]):
        dense += jnp.where(ids[k : k + 1] == place % half, share[k : k + 1], 0.0)
    high = dense.astype(jnp.bfloat16).astype(jnp.float32)
    terms = jnp.where(place < half, high, dense - high).astype(jnp.bfloat16)
    row = lax.broadcasted_iota(jnp.int32, (tokens, tokens), 0)
    column = lax.broadcasted_iota(jnp.int32, (tokens, tokens), 1)
    one = jnp.where(row == column, 1.0, 0.0).astype(jnp.bfloat16)
    upright = lax.dot_general(one, terms, (((1,), (1,)), ((), ())), preferred_element_type=jnp.float32)
    message_ref[:, :width] = states_ref[...]
    message_ref[:, width:] = upright.astype(jnp.bfloat16)


def make_message(states, ids, probs, step, tail):
    _, tokens, width = states.shape
    states, ids, probs = (pltpu.with_memory_space_constraint(x, pltpu.HBM) for x in (states, ids, probs))

    def of_step(x):
        return pl.BlockSpec((None,) + x.shape[1:], lambda i: (step, 0, 0))

    return pl.pallas_call(
        message_kernel,
        grid=(1,),
        out_shape=jax.ShapeDtypeStruct((tokens, width + tail), jnp.bfloat16),
        in_specs=[of_step(states), of_step(ids), of_step(probs)],
        out_specs=pl.BlockSpec((tokens, width + tail), lambda i: (0, 0)),
        compiler_params=pltpu.CompilerParams(vmem_limit_bytes=4 * MIB),
        name="message",
    )(states, ids, probs)


def load_kernel(*refs):
    count = len(refs) // 3
    copies = [
        pltpu.make_async_copy(refs[i], refs[count + i], refs[2 * count + i]) for i in range(count)
    ]
    for copy in copies:
        copy.start()
    for copy in copies:
        copy.wait()


def load_weights(*arrays):
    arrays = [pltpu.with_memory_space_constraint(x, pltpu.HBM) for x in arrays]
    return pl.pallas_call(
        load_kernel,
        out_shape=[pltpu.VMEM(x.shape, x.dtype) for x in arrays],
        in_specs=[pl.BlockSpec(memory_space=pltpu.HBM)] * len(arrays),
        out_specs=[in_vmem()] * len(arrays),
        scratch_shapes=[pltpu.SemaphoreType.DMA(())] * len(arrays),
        cost_estimate=pl.CostEstimate(
            flops=0, bytes_accessed=sum(2 * x.size for x in arrays), transcendentals=0
        ),
        compiler_params=pltpu.CompilerParams(vmem_limit_bytes=4 * MIB),
        name="load_weights",
    )(*arrays)


def expert_kernel(swapped, count, flags_ref, gate_ref, up_ref, down_ref, *refs):
    *sources, own_ref, near_ref, other_ref, rows, hidden = refs
    width, units = gate_ref.shape
    tail = rows.shape[1] - width
    owner = lax.axis_index("expert")
    slot = jnp.bitwise_xor(owner, flags_ref[owner]) if swapped else owner
    at = 0
    for source in sources:
        rows[at : at + source.shape[0]] = source[...]
        at += source.shape[0]
    total = rows.shape[0]
    lane = lax.broadcasted_iota(jnp.int32, (total, tail), 1)
    terms = rows[:, width:].astype(jnp.float32)
    weight = jnp.sum(jnp.where(lane % (tail // 2) == slot, terms, 0.0), axis=1, keepdims=True)
    step = 256
    for at in range(0, units, step):
        gate = jnp.dot(rows[:, :width], gate_ref[:, at : at + step], preferred_element_type=jnp.float32)
        up = jnp.dot(rows[:, :width], up_ref[:, at : at + step], preferred_element_type=jnp.float32)
        value = gate / (1.0 + jnp.exp(-gate)) * up
        hidden[:, at : at + step] = (value * weight).astype(jnp.bfloat16)

    def columns(index, _):
        at = pl.ds(pl.multiple_of(index * 512, 512), 512)
        out = jnp.dot(hidden[...], down_ref[:, at], preferred_element_type=jnp.float32)
        out = out.astype(jnp.bfloat16)
        own_ref[:, at] = out[:count]
        near_ref[:, at] = out[count : 2 * count]
        other_ref[:, at] = out[2 * count :]
        return 0

    lax.fori_loop(0, width // 512, columns, 0)


def run_expert(swapped, flags, weights, parts):
    total = sum(part.shape[0] for part in parts)
    count = total // 4
    width, units = weights[0].shape
    weights = [pltpu.with_memory_space_constraint(w, pltpu.VMEM) for w in weights]
    return pl.pallas_call(
        functools.partial(expert_kernel, swapped, count),
        out_shape=[jax.ShapeDtypeStruct((k * count, width), jnp.bfloat16) for k in (1, 1, 2)],
        in_specs=[pl.BlockSpec(memory_space=pltpu.SMEM)] + [in_vmem()] * (3 + len(parts)),
        out_specs=[in_vmem()] * 3,
        scratch_shapes=[
            pltpu.VMEM((total, parts[0].shape[1]), jnp.bfloat16),
            pltpu.VMEM((total, units), jnp.bfloat16),
        ],
        compiler_params=pltpu.CompilerParams(vmem_limit_bytes=16 * MIB),
        cost_estimate=pl.CostEstimate(
            flops=total * width * units * 6, bytes_accessed=4 * total * width, transcendentals=0
        ),
        name="expert",
    )(flags, *weights, *parts)


def on_device(states, ids, probs, flags, w_gate, w_up, w_down):
    devices = lax.axis_size("expert")
    lines = devices // 4
    steps, tokens, width = states.shape

    def index(far, near, core):
        return far * 4 + near * 2 + core

    every = [(z, y, c) for z in range(lines) for y in range(2) for c in range(2)]

    def swap_core(x):
        return lax.ppermute(x, "expert", [(index(z, y, c), index(z, y, 1 - c)) for z, y, c in every])

    def swap_near(x):
        return lax.ppermute(x, "expert", [(index(z, y, c), index(z, 1 - y, c)) for z, y, c in every])

    def shift_far(x, by):
        return lax.ppermute(x, "expert", [(index(z, y, c), index((z + by) % lines, y, c)) for z, y, c in every])

    tail = 2 * devices
    tail = -(-tail // LANES) * LANES
    ids, probs = jnp.swapaxes(ids, 1, 2), jnp.swapaxes(probs, 1, 2)
    order = sorted(range(lines), key=lambda by: min(by, lines - by))
    close, far = order[1 : 1 + lines // 2], order[1 + lines // 2 :]
    weights = load_weights(w_gate[0], w_up[0], w_down[0])
    messages = [make_message(states, ids, probs, step, tail) for step in range(steps)]
    gathered = []
    blocks = None
    for step in range(steps):
        message = messages[step]
        near_own = swap_near(message)
        if step:
            message, _ = lax.optimization_barrier((message, blocks))
        blocks = [shift_far(message, by) for by in order[1:]]
        if not step:
            blocks, weights, messages[1:] = lax.optimization_barrier((blocks, weights, messages[1:]))
            split = len(close)
            near = [near_own, swap_near(jnp.concatenate(blocks[:split])), swap_near(jnp.concatenate(blocks[split:]))]
            core = [swap_core(jnp.concatenate(near[:2])), swap_core(near[2])]
        else:
            near = [near_own, swap_near(jnp.concatenate(blocks))]
            core = [swap_core(jnp.concatenate(near))]
        line = [message, *blocks]
        gathered.append((*line, *near, swap_core(jnp.concatenate(line)), *core))
    outputs = []
    other = None
    for step in range(steps):
        parts = gathered[step]
        if step:
            parts, _ = lax.optimization_barrier((parts, other))
        own, peer, other = run_expert(step > 0, flags, weights, parts)
        other = swap_core(other)
        half = own.shape[0]
        own = own.astype(jnp.float32) + other[:half].astype(jnp.float32)
        peer = (peer.astype(jnp.float32) + other[half:].astype(jnp.float32)).astype(jnp.bfloat16)
        cuts = [0, half] if step + 1 < steps else [0, tokens, (1 + len(close)) * tokens, half]
        places = list(zip(cuts[:-1], cuts[1:]))
        blocks = []
        for low, high in places[::-1]:
            near = swap_near(peer[low:high])
            both = own[low:high] + near.astype(jnp.float32)
            blocks = [both[at : at + tokens] for at in range(0, high - low, tokens)] + blocks
        mixed = blocks[0]
        for by, block in zip(order[1:], blocks[1:]):
            mixed += shift_far(block.astype(jnp.bfloat16), lines - by).astype(jnp.float32)
        outputs.append(mixed.astype(jnp.bfloat16))
    return jnp.stack(outputs)


def solution(mesh):
    rows = P(None, ("groups", "expert"), None)
    weights = P("expert", None, None)
    return jax.shard_map(
        on_device,
        mesh=mesh,
        in_specs=(rows, rows, rows, P(), weights, weights, weights),
        out_specs=rows,
        check_vma=False,
    )
```

```python
import functools

import jax
import jax.numpy as jnp
from jax import lax
from jax.experimental import pallas as pl
from jax.experimental.pallas import tpu as pltpu
from jax.sharding import PartitionSpec as P

LANES = 128
MIB = 1 << 20


def in_vmem():
    return pl.BlockSpec(memory_space=pltpu.VMEM)


def message_kernel(states_ref, ids_ref, probs_ref, message_ref):
    tokens, width = states_ref.shape
    tail = message_ref.shape[1] - width
    half = tail // 2
    probs = probs_ref[...]
    share = probs / jnp.sum(probs, axis=0, keepdims=True)
    ids = ids_ref[...]
    place = lax.broadcasted_iota(jnp.int32, (tail, tokens), 0)
    dense = jnp.zeros((tail, tokens), jnp.float32)
    for k in range(ids.shape[0]):
        dense += jnp.where(ids[k : k + 1] == place % half, share[k : k + 1], 0.0)
    high = dense.astype(jnp.bfloat16).astype(jnp.float32)
    terms = jnp.where(place < half, high, dense - high).astype(jnp.bfloat16)
    row = lax.broadcasted_iota(jnp.int32, (tokens, tokens), 0)
    column = lax.broadcasted_iota(jnp.int32, (tokens, tokens), 1)
    one = jnp.where(row == column, 1.0, 0.0).astype(jnp.bfloat16)
    upright = lax.dot_general(one, terms, (((1,), (1,)), ((), ())), preferred_element_type=jnp.float32)
    message_ref[:, :width] = states_ref[...]
    message_ref[:, width:] = upright.astype(jnp.bfloat16)


def make_message(states, ids, probs, step, tail):
    _, tokens, width = states.shape
    states, ids, probs = (pltpu.with_memory_space_constraint(x, pltpu.HBM) for x in (states, ids, probs))

    def of_step(x):
        return pl.BlockSpec((None,) + x.shape[1:], lambda i: (step, 0, 0))

    return pl.pallas_call(
        message_kernel,
        grid=(1,),
        out_shape=jax.ShapeDtypeStruct((tokens, width + tail), jnp.bfloat16),
        in_specs=[of_step(states), of_step(ids), of_step(probs)],
        out_specs=pl.BlockSpec((tokens, width + tail), lambda i: (0, 0)),
        compiler_params=pltpu.CompilerParams(vmem_limit_bytes=4 * MIB),
        name="message",
    )(states, ids, probs)


def load_kernel(*refs):
    count = len(refs) // 3
    copies = [
        pltpu.make_async_copy(refs[i], refs[count + i], refs[2 * count + i]) for i in range(count)
    ]
    for copy in copies:
        copy.start()
    for copy in copies:
        copy.wait()


def load_weights(*arrays):
    arrays = [pltpu.with_memory_space_constraint(x, pltpu.HBM) for x in arrays]
    return pl.pallas_call(
        load_kernel,
        out_shape=[pltpu.VMEM(x.shape, x.dtype) for x in arrays],
        in_specs=[pl.BlockSpec(memory_space=pltpu.HBM)] * len(arrays),
        out_specs=[in_vmem()] * len(arrays),
        scratch_shapes=[pltpu.SemaphoreType.DMA(())] * len(arrays),
        cost_estimate=pl.CostEstimate(
            flops=0, bytes_accessed=sum(2 * x.size for x in arrays), transcendentals=0
        ),
        compiler_params=pltpu.CompilerParams(vmem_limit_bytes=4 * MIB),
        name="load_weights",
    )(*arrays)


def expert_kernel(swapped, count, plan, flags_ref, gate_ref, up_ref, down_ref, *refs):
    *sources, own_ref, near_ref, other_ref, rows, hidden = refs
    width, units = gate_ref.shape
    tail = rows.shape[1] - width
    owner = lax.axis_index("expert")
    slot = jnp.bitwise_xor(owner, flags_ref[owner]) if swapped else owner
    at = 0
    for source, low, high in plan:
        rows[at : at + high - low] = sources[source][low:high]
        at += high - low
    total = rows.shape[0]
    lane = lax.broadcasted_iota(jnp.int32, (total, tail), 1)
    terms = rows[:, width:].astype(jnp.float32)
    weight = jnp.sum(jnp.where(lane % (tail // 2) == slot, terms, 0.0), axis=1, keepdims=True)
    step = 256
    for at in range(0, units, step):
        gate = jnp.dot(rows[:, :width], gate_ref[:, at : at + step], preferred_element_type=jnp.float32)
        up = jnp.dot(rows[:, :width], up_ref[:, at : at + step], preferred_element_type=jnp.float32)
        value = gate / (1.0 + jnp.exp(-gate)) * up
        hidden[:, at : at + step] = (value * weight).astype(jnp.bfloat16)

    def columns(index, _):
        at = pl.ds(pl.multiple_of(index * 512, 512), 512)
        out = jnp.dot(hidden[...], down_ref[:, at], preferred_element_type=jnp.float32)
        out = out.astype(jnp.bfloat16)
        own_ref[:, at] = out[:count]
        near_ref[:, at] = out[count : 2 * count]
        other_ref[:, at] = out[2 * count :]
        return 0

    lax.fori_loop(0, width // 512, columns, 0)


def run_expert(swapped, flags, weights, parts, plan):
    total = sum(high - low for _, low, high in plan)
    count = total // 4
    width, units = weights[0].shape
    weights = [pltpu.with_memory_space_constraint(w, pltpu.VMEM) for w in weights]
    return pl.pallas_call(
        functools.partial(expert_kernel, swapped, count, plan),
        out_shape=[jax.ShapeDtypeStruct((k * count, width), jnp.bfloat16) for k in (1, 1, 2)],
        in_specs=[pl.BlockSpec(memory_space=pltpu.SMEM)] + [in_vmem()] * (3 + len(parts)),
        out_specs=[in_vmem()] * 3,
        scratch_shapes=[
            pltpu.VMEM((total, parts[0].shape[1]), jnp.bfloat16),
            pltpu.VMEM((total, units), jnp.bfloat16),
        ],
        compiler_params=pltpu.CompilerParams(vmem_limit_bytes=16 * MIB),
        cost_estimate=pl.CostEstimate(
            flops=total * width * units * 6, bytes_accessed=4 * total * width, transcendentals=0
        ),
        name="expert",
    )(flags, *weights, *parts)


def on_device(states, ids, probs, flags, w_gate, w_up, w_down):
    devices = lax.axis_size("expert")
    lines = devices // 4
    steps, tokens, width = states.shape

    def index(far, near, core):
        return far * 4 + near * 2 + core

    every = [(z, y, c) for z in range(lines) for y in range(2) for c in range(2)]

    def swap_core(x):
        return lax.ppermute(x, "expert", [(index(z, y, c), index(z, y, 1 - c)) for z, y, c in every])

    def swap_near(x):
        return lax.ppermute(x, "expert", [(index(z, y, c), index(z, 1 - y, c)) for z, y, c in every])

    def swap_far(x, by):
        return lax.ppermute(x, "expert", [(index(z, y, c), index(z ^ by, y, c)) for z, y, c in every])

    def stack(blocks):
        return jnp.concatenate(blocks) if len(blocks) > 1 else blocks[0]

    tail = 2 * devices
    tail = -(-tail // LANES) * LANES
    ids, probs = jnp.swapaxes(ids, 1, 2), jnp.swapaxes(probs, 1, 2)
    middle = lines // 2
    head, half = middle * tokens, lines * tokens
    plan = (
        *((0, 0, head), (1, 0, head), (0, head, half), (2, 0, head)),
        *((3, 0, head), (4, 0, head), (3, head, half), (5, 0, head)),
    )
    messages = [make_message(states, ids, probs, step, tail) for step in range(steps)]
    weights = [w_gate[0], w_up[0], w_down[0]]
    near_owns = [swap_near(message) for message in messages]
    gathered, far = [], None
    for step in range(steps):
        message, near_own = messages[step], near_owns[step]
        if step:
            message, _ = lax.optimization_barrier((message, far))
        close = stack([swap_far(message, by) for by in range(1, middle)])
        far = [swap_far(message, by) for by in range(middle, lines)]
        near_close = swap_near(close)
        if not step:
            weights, close = lax.optimization_barrier((weights, close))
            weights = load_weights(*weights)
            far, weights, near_close, near_owns = lax.optimization_barrier((far, weights, near_close, near_owns))
        far = stack(far)
        near_far = swap_near(far)
        line = jnp.concatenate([message, close, near_own, near_close])
        gathered.append((line, far, near_far, swap_core(line), swap_core(far), swap_core(near_far)))
    outputs = []
    for step in range(steps):
        parts = gathered[step]
        if step:
            parts, _ = lax.optimization_barrier((parts, ready))
        own, peer, other = run_expert(step > 0, flags, weights, parts, plan)
        other = swap_core(other)
        own = own.astype(jnp.float32) + other[:half].astype(jnp.float32)
        peer = (peer.astype(jnp.float32) + other[half:].astype(jnp.float32)).astype(jnp.bfloat16)
        ready = peer
        near_far = swap_near(peer[head:])
        near_close = peer[:head]
        if step + 1 == steps:
            near_close, _ = lax.optimization_barrier((near_close, near_far))
        far = own[head:] + near_far.astype(jnp.float32)
        _, close = lax.optimization_barrier((far, swap_near(near_close)))
        close = own[:head] + close.astype(jnp.float32)
        mixed = close[:tokens]
        for by in range(lines - 1, 0, -1):
            block = far[by * tokens - head :][:tokens] if by >= middle else close[by * tokens :][:tokens]
            mixed += swap_far(block.astype(jnp.bfloat16), by).astype(jnp.float32)
        outputs.append(mixed.astype(jnp.bfloat16))
    return jnp.stack(outputs)


def solution(mesh):
    rows = P(None, ("groups", "expert"), None)
    weights = P("expert", None, None)
    return jax.shard_map(
        on_device,
        mesh=mesh,
        in_specs=(rows, rows, rows, P(), weights, weights, weights),
        out_specs=rows,
        check_vma=False,
    )
```

```python
import functools

import jax
import jax.numpy as jnp
from jax import lax
from jax.experimental import pallas as pl
from jax.experimental.pallas import tpu as pltpu
from jax.sharding import PartitionSpec as P

LANES = 128
MIB = 1 << 20


def in_vmem():
    return pl.BlockSpec(memory_space=pltpu.VMEM)


def message_kernel(states_ref, ids_ref, probs_ref, *message_refs):
    steps, tokens, width = states_ref.shape
    tail = message_refs[0].shape[1] - width
    half = tail // 2
    place = lax.broadcasted_iota(jnp.int32, (tail, tokens), 0)
    row = lax.broadcasted_iota(jnp.int32, (tokens, tokens), 0)
    column = lax.broadcasted_iota(jnp.int32, (tokens, tokens), 1)
    one = jnp.where(row == column, 1.0, 0.0).astype(jnp.bfloat16)
    for step in range(steps):
        probs = probs_ref[step]
        share = probs / jnp.sum(probs, axis=0, keepdims=True)
        ids = ids_ref[step]
        dense = jnp.zeros((tail, tokens), jnp.float32)
        for k in range(ids.shape[0]):
            dense += jnp.where(ids[k : k + 1] == place % half, share[k : k + 1], 0.0)
        high = dense.astype(jnp.bfloat16).astype(jnp.float32)
        terms = jnp.where(place < half, high, dense - high).astype(jnp.bfloat16)
        upright = lax.dot_general(one, terms, (((1,), (1,)), ((), ())), preferred_element_type=jnp.float32)
        upright = upright.astype(jnp.bfloat16)
        for message_ref, at in ((message_refs[0], step * tokens), (message_refs[step + 1], 0)):
            message_ref[at : at + tokens, :width] = states_ref[step]
            message_ref[at : at + tokens, width:] = upright


def make_messages(states, ids, probs, tail):
    steps, tokens, width = states.shape
    states, ids, probs = (pltpu.with_memory_space_constraint(x, pltpu.HBM) for x in (states, ids, probs))

    def whole(shape):
        return pl.BlockSpec(shape, lambda i: (0,) * len(shape))

    shapes = [(steps * tokens, width + tail)] + [(tokens, width + tail)] * steps
    return pl.pallas_call(
        message_kernel,
        grid=(1,),
        out_shape=[jax.ShapeDtypeStruct(shape, jnp.bfloat16) for shape in shapes],
        in_specs=[whole(x.shape) for x in (states, ids, probs)],
        out_specs=[whole(shape) for shape in shapes],
        compiler_params=pltpu.CompilerParams(vmem_limit_bytes=4 * MIB),
        name="messages",
    )(states, ids, probs)


def load_kernel(*refs):
    count = len(refs) // 3
    copies = [
        pltpu.make_async_copy(refs[i], refs[count + i], refs[2 * count + i]) for i in range(count)
    ]
    for copy in copies:
        copy.start()
    for copy in copies:
        copy.wait()


def load_weights(*arrays):
    arrays = [pltpu.with_memory_space_constraint(x, pltpu.HBM) for x in arrays]
    return pl.pallas_call(
        load_kernel,
        out_shape=[pltpu.VMEM(x.shape, x.dtype) for x in arrays],
        in_specs=[pl.BlockSpec(memory_space=pltpu.HBM)] * len(arrays),
        out_specs=[in_vmem()] * len(arrays),
        scratch_shapes=[pltpu.SemaphoreType.DMA(())] * len(arrays),
        cost_estimate=pl.CostEstimate(flops=0, bytes_accessed=0, transcendentals=0),
        compiler_params=pltpu.CompilerParams(vmem_limit_bytes=4 * MIB),
        name="load_weights",
    )(*arrays)


def expert_kernel(swapped, count, plan, flags_ref, gate_ref, up_ref, down_ref, *refs):
    *sources, own_ref, near_ref, other_ref, rows, hidden = refs
    width, units = gate_ref.shape
    tail = rows.shape[1] - width
    owner = lax.axis_index("expert")
    slot = jnp.bitwise_xor(owner, flags_ref[owner]) if swapped else owner
    at = 0
    for source, low, high in plan:
        rows[at : at + high - low] = sources[source][low:high]
        at += high - low
    total = rows.shape[0]
    lane = lax.broadcasted_iota(jnp.int32, (total, tail), 1)
    terms = rows[:, width:].astype(jnp.float32)
    weight = jnp.sum(jnp.where(lane % (tail // 2) == slot, terms, 0.0), axis=1, keepdims=True)
    step = 256
    for at in range(0, units, step):
        gate = jnp.dot(rows[:, :width], gate_ref[:, at : at + step], preferred_element_type=jnp.float32)
        up = jnp.dot(rows[:, :width], up_ref[:, at : at + step], preferred_element_type=jnp.float32)
        value = gate / (1.0 + jnp.exp(-gate)) * up
        hidden[:, at : at + step] = (value * weight).astype(jnp.bfloat16)

    def columns(index, _):
        at = pl.ds(pl.multiple_of(index * 512, 512), 512)
        out = jnp.dot(hidden[...], down_ref[:, at], preferred_element_type=jnp.float32)
        out = out.astype(jnp.bfloat16)
        own_ref[:, at] = out[:count]
        near_ref[:, at] = out[count : 2 * count]
        other_ref[:, at] = out[2 * count :]
        return 0

    lax.fori_loop(0, width // 512, columns, 0)


def run_expert(swapped, flags, weights, parts, plan):
    total = sum(high - low for _, low, high in plan)
    count = total // 4
    width, units = weights[0].shape
    weights = [pltpu.with_memory_space_constraint(w, pltpu.VMEM) for w in weights]
    return pl.pallas_call(
        functools.partial(expert_kernel, swapped, count, plan),
        out_shape=[jax.ShapeDtypeStruct((k * count, width), jnp.bfloat16) for k in (1, 1, 2)],
        in_specs=[pl.BlockSpec(memory_space=pltpu.SMEM)] + [in_vmem()] * (3 + len(parts)),
        out_specs=[in_vmem()] * 3,
        scratch_shapes=[
            pltpu.VMEM((total, parts[0].shape[1]), jnp.bfloat16),
            pltpu.VMEM((total, units), jnp.bfloat16),
        ],
        compiler_params=pltpu.CompilerParams(vmem_limit_bytes=16 * MIB),
        cost_estimate=pl.CostEstimate(flops=0, bytes_accessed=0, transcendentals=0),
        name="expert",
    )(flags, *weights, *parts)


def on_device(states, ids, probs, flags, w_gate, w_up, w_down):
    devices = lax.axis_size("expert")
    lines = devices // 4
    steps, tokens, width = states.shape

    def index(far, near, core):
        return far * 4 + near * 2 + core

    every = [(z, y, c) for z in range(lines) for y in range(2) for c in range(2)]

    def swap_core(x):
        return lax.ppermute(x, "expert", [(index(z, y, c), index(z, y, 1 - c)) for z, y, c in every])

    def swap_near(x):
        return lax.ppermute(x, "expert", [(index(z, y, c), index(z, 1 - y, c)) for z, y, c in every])

    def swap_far(x, by):
        return lax.ppermute(x, "expert", [(index(z, y, c), index(z ^ by, y, c)) for z, y, c in every])

    tail = 2 * devices
    tail = -(-tail // LANES) * LANES
    ids, probs = jnp.swapaxes(ids, 1, 2), jnp.swapaxes(probs, 1, 2)
    strides = [lines >> shift for shift in range(1, lines.bit_length())]
    half = lines * tokens
    message, *own_messages = make_messages(states, ids, probs, tail)
    near_message = swap_near(message)
    w_gate, w_up, w_down = w_gate[0], w_up[0], w_down[0]
    pieces, nears, held = [[] for _ in range(steps)], [[] for _ in range(steps)], own_messages
    for place, by in enumerate(strides):
        for step in range(steps):
            mine = held[step]
            if step:
                mine, _ = lax.optimization_barrier((mine, pieces[step - 1][place]))
            piece = swap_far(mine, by)
            if not step and not place:
                loaded = load_weights(w_gate, w_up)
                piece, loaded, near_message = lax.optimization_barrier((piece, loaded, near_message))
            if step == 1 and not place:
                w_down, _ = lax.optimization_barrier((w_down, pieces[0][0]))
                loaded += load_weights(w_down)
                piece, loaded = lax.optimization_barrier((piece, loaded))
            pieces[step].append(piece)
            nears[step].append(swap_near(piece))
            if place + 1 < len(strides):
                held[step] = jnp.concatenate([held[step], piece])
    weights = loaded
    shared = jnp.concatenate([message, near_message, *pieces[0][:-1], *nears[0][:-1]])
    shared = [shared, swap_core(shared)]
    outputs, ready = [], None
    for step in range(steps):
        blocks, near = pieces[step][-1], nears[step][-1]
        parts = [*shared, blocks, near, swap_core(blocks), swap_core(near)]
        if step:
            own = jnp.concatenate([*pieces[step][:-1], *nears[step][:-1]])
            parts += [own, swap_core(own)]
        plan = []
        some = half // 2 - tokens
        for core in range(2):
            for side in range(2):
                at = (side * steps + step) * tokens
                plan.append((core, at, at + tokens))
                at = side * some + (0 if step else 2 * steps * tokens)
                plan.append((core + 6 if step else core, at, at + some))
                plan.append((2 + 2 * core + side, 0, half // 2))
        parts, _ = lax.optimization_barrier((parts, ready if step else pieces))
        own, peer, other = run_expert(step > 0, flags, weights, parts, tuple(plan))
        other, _ = lax.optimization_barrier((other, near_high if step else nears[1][-1]))
        other = swap_core(other)
        own = own.astype(jnp.float32) + other[:half].astype(jnp.float32)
        peer = (peer.astype(jnp.float32) + other[half:].astype(jnp.float32)).astype(jnp.bfloat16)
        ready = peer
        size = half // 2
        near_high, near_low = swap_near(peer[size:]), peer[:size]
        if step + 1 == steps:
            near_low, _ = lax.optimization_barrier((near_low, near_high))
        high = own[size:] + near_high.astype(jnp.float32)
        _, near_low = lax.optimization_barrier((high, swap_near(near_low)))
        line = own[:size] + near_low.astype(jnp.float32)
        for by in strides[::-1]:
            line += swap_far(high.astype(jnp.bfloat16), by).astype(jnp.float32)
            size //= 2
            line, high = line[:size], line[size:]
        outputs.append(jnp.concatenate([line, high]).astype(jnp.bfloat16))
    return jnp.stack(outputs)


def solution(mesh):
    rows = P(None, ("groups", "expert"), None)
    weights = P("expert", None, None)
    return jax.shard_map(
        on_device,
        mesh=mesh,
        in_specs=(rows, rows, rows, P(), weights, weights, weights),
        out_specs=rows,
        check_vma=False,
    )
```

```python
import functools

import jax
import jax.numpy as jnp
from jax import lax
from jax.experimental import pallas as pl
from jax.experimental.pallas import tpu as pltpu
from jax.sharding import PartitionSpec as P

LANES = 128
MIB = 1 << 20


def in_vmem():
    return pl.BlockSpec(memory_space=pltpu.VMEM)


def message_kernel(states_ref, ids_ref, probs_ref, *message_refs):
    steps, tokens, width = states_ref.shape
    tail = message_refs[0].shape[1] - width
    half = tail // 2
    place = lax.broadcasted_iota(jnp.int32, (tail, tokens), 0)
    row = lax.broadcasted_iota(jnp.int32, (tokens, tokens), 0)
    column = lax.broadcasted_iota(jnp.int32, (tokens, tokens), 1)
    one = jnp.where(row == column, 1.0, 0.0).astype(jnp.bfloat16)
    for step in range(steps):
        probs = probs_ref[step]
        share = probs / jnp.sum(probs, axis=0, keepdims=True)
        ids = ids_ref[step]
        dense = jnp.zeros((tail, tokens), jnp.float32)
        for k in range(ids.shape[0]):
            dense += jnp.where(ids[k : k + 1] == place % half, share[k : k + 1], 0.0)
        high = dense.astype(jnp.bfloat16).astype(jnp.float32)
        terms = jnp.where(place < half, high, dense - high).astype(jnp.bfloat16)
        upright = lax.dot_general(one, terms, (((1,), (1,)), ((), ())), preferred_element_type=jnp.float32)
        upright = upright.astype(jnp.bfloat16)
        for message_ref, at in ((message_refs[0], step * tokens), (message_refs[step + 1], 0)):
            message_ref[at : at + tokens, :width] = states_ref[step]
            message_ref[at : at + tokens, width:] = upright


def make_messages(states, ids, probs, tail):
    steps, tokens, width = states.shape
    states, ids, probs = (pltpu.with_memory_space_constraint(x, pltpu.HBM) for x in (states, ids, probs))

    def whole(shape):
        return pl.BlockSpec(shape, lambda i: (0,) * len(shape))

    shapes = [(steps * tokens, width + tail)] + [(tokens, width + tail)] * steps
    return pl.pallas_call(
        message_kernel,
        grid=(1,),
        out_shape=[jax.ShapeDtypeStruct(shape, jnp.bfloat16) for shape in shapes],
        in_specs=[whole(x.shape) for x in (states, ids, probs)],
        out_specs=[whole(shape) for shape in shapes],
        compiler_params=pltpu.CompilerParams(vmem_limit_bytes=4 * MIB),
        name="messages",
    )(states, ids, probs)


def load_kernel(*refs):
    count = len(refs) // 3
    copies = [
        pltpu.make_async_copy(refs[i], refs[count + i], refs[2 * count + i]) for i in range(count)
    ]
    for copy in copies:
        copy.start()
    for copy in copies:
        copy.wait()


def load_weights(*arrays):
    arrays = [pltpu.with_memory_space_constraint(x, pltpu.HBM) for x in arrays]
    return pl.pallas_call(
        load_kernel,
        out_shape=[pltpu.VMEM(x.shape, x.dtype) for x in arrays],
        in_specs=[pl.BlockSpec(memory_space=pltpu.HBM)] * len(arrays),
        out_specs=[in_vmem()] * len(arrays),
        scratch_shapes=[pltpu.SemaphoreType.DMA(())] * len(arrays),
        cost_estimate=pl.CostEstimate(flops=0, bytes_accessed=0, transcendentals=0),
        compiler_params=pltpu.CompilerParams(vmem_limit_bytes=4 * MIB),
        name="load_weights",
    )(*arrays)


def expert_kernel(swapped, count, plan, flags_ref, gate_ref, up_ref, down_ref, *refs):
    *sources, own_ref, near_ref, other_ref, rows, hidden = refs
    width, units = gate_ref.shape
    tail = rows.shape[1] - width
    owner = lax.axis_index("expert")
    slot = jnp.bitwise_xor(owner, flags_ref[owner]) if swapped else owner
    at = 0
    for source, low, high in plan:
        rows[at : at + high - low] = sources[source][low:high]
        at += high - low
    total = rows.shape[0]
    lane = lax.broadcasted_iota(jnp.int32, (total, tail), 1)
    terms = rows[:, width:].astype(jnp.float32)
    weight = jnp.sum(jnp.where(lane % (tail // 2) == slot, terms, 0.0), axis=1, keepdims=True)
    step = 256
    for at in range(0, units, step):
        gate = jnp.dot(rows[:, :width], gate_ref[:, at : at + step], preferred_element_type=jnp.float32)
        up = jnp.dot(rows[:, :width], up_ref[:, at : at + step], preferred_element_type=jnp.float32)
        value = gate / (1.0 + jnp.exp(-gate)) * up
        hidden[:, at : at + step] = (value * weight).astype(jnp.bfloat16)

    def columns(index, _):
        at = pl.ds(pl.multiple_of(index * 512, 512), 512)
        out = jnp.dot(hidden[...], down_ref[:, at], preferred_element_type=jnp.float32)
        out = out.astype(jnp.bfloat16)
        own_ref[:, at] = out[:count]
        near_ref[:, at] = out[count : 2 * count]
        other_ref[:, at] = out[2 * count :]
        return 0

    lax.fori_loop(0, width // 512, columns, 0)


def run_expert(swapped, flags, weights, parts, plan):
    total = sum(high - low for _, low, high in plan)
    count = total // 4
    width, units = weights[0].shape
    weights = [pltpu.with_memory_space_constraint(w, pltpu.VMEM) for w in weights]
    return pl.pallas_call(
        functools.partial(expert_kernel, swapped, count, plan),
        out_shape=[jax.ShapeDtypeStruct((k * count, width), jnp.bfloat16) for k in (1, 1, 2)],
        in_specs=[pl.BlockSpec(memory_space=pltpu.SMEM)] + [in_vmem()] * (3 + len(parts)),
        out_specs=[in_vmem()] * 3,
        scratch_shapes=[
            pltpu.VMEM((total, parts[0].shape[1]), jnp.bfloat16),
            pltpu.VMEM((total, units), jnp.bfloat16),
        ],
        compiler_params=pltpu.CompilerParams(vmem_limit_bytes=16 * MIB),
        cost_estimate=pl.CostEstimate(flops=0, bytes_accessed=0, transcendentals=0),
        name="expert",
    )(flags, *weights, *parts)


def on_device(states, ids, probs, flags, w_gate, w_up, w_down):
    devices = lax.axis_size("expert")
    lines = devices // 4
    steps, tokens, width = states.shape

    def index(far, near, core):
        return far * 4 + near * 2 + core

    every = [(z, y, c) for z in range(lines) for y in range(2) for c in range(2)]

    def swap_core(x):
        return lax.ppermute(x, "expert", [(index(z, y, c), index(z, y, 1 - c)) for z, y, c in every])

    def swap_near(x):
        return lax.ppermute(x, "expert", [(index(z, y, c), index(z, 1 - y, c)) for z, y, c in every])

    def swap_far(x, by):
        return lax.ppermute(x, "expert", [(index(z, y, c), index(z ^ by, y, c)) for z, y, c in every])

    tail = 2 * devices
    tail = -(-tail // LANES) * LANES
    ids, probs = jnp.swapaxes(ids, 1, 2), jnp.swapaxes(probs, 1, 2)
    middle = lines // 2
    strides = [middle >> shift for shift in range(1, middle.bit_length())]
    head, half = middle * tokens, lines * tokens

    def grow(block):
        for by in strides:
            block = jnp.concatenate([block, swap_far(block, by)])
        return block

    def collapse(block):
        for by in strides[::-1]:
            keep = block.shape[0] // 2
            block = block[:keep] + swap_far(block[keep:].astype(jnp.bfloat16), by).astype(jnp.float32)
        return block

    def after(x, *events):
        return lax.optimization_barrier((x, events))[0]

    def of_step(x, step):
        return jnp.concatenate([x[at : at + tokens] for at in range(step * tokens, x.shape[0], steps * tokens)])

    w_gate, w_up, w_down = w_gate[0], w_up[0], w_down[0]
    message, *own_messages = make_messages(states, ids, probs, tail)
    near_message = swap_near(message)
    close = message
    received = []
    for by in strides:
        received.append(swap_far(close, by))
        close = jnp.concatenate([close, received[-1]])
    cross = swap_far(own_messages[0], middle)
    loaded = load_weights(w_gate, w_up)
    received, cross, near_message, loaded = lax.optimization_barrier((received, cross, near_message, loaded))
    close = jnp.concatenate([message, *received])
    far, near_far = [], []
    for step in range(steps):
        if step:
            far.append(grow(crossed))
            near_far.append(swap_near(jnp.concatenate([far[step], of_step(close, step)[tokens:]])))
            if step + 1 < steps:
                crossed = swap_far(after(own_messages[step + 1], crossed), middle)
        else:
            near = swap_near(of_step(close, step)[tokens:])
            if steps > 1:
                crossed = swap_far(after(own_messages[1], cross), middle)
            far.append(grow(cross))
            w_down = after(w_down, cross)
            last = load_weights(w_down)
            far[0], near, last = lax.optimization_barrier((far[0], near, last))
            loaded += last
            near_close = near
            near_far.append(swap_near(far[0]))
    shared = jnp.concatenate([close, near_message, near_close])
    shared = [shared, swap_core(shared)]
    outputs, ready = [], far
    for step in range(steps):
        if step:
            rest = jnp.concatenate([far[step], near_far[step]])
            parts = [*shared, rest, swap_core(rest)]
        else:
            parts = [*shared, far[0], swap_core(after(far[0], crossed)), near_far[0], swap_core(near_far[0])]
        plan = []
        for core in range(2):
            for by in range(middle):
                at = (by * steps + step) * tokens
                plan.append((core, at, at + tokens))
            plan.append((2 + core, 0, head))
            at = (middle * steps + step) * tokens
            plan.append((core, at, at + tokens))
            at = 2 * head if step else (middle + 1) * steps * tokens
            plan.append((2 * (step > 0) + core, at, at + head - tokens))
            at = head if step else 0
            plan.append(((2 if step else 4) + core, at, at + head))
        own, peer, other = run_expert(step > 0, flags, loaded, after(parts, ready), tuple(plan))
        other = swap_core(after(other, near_high if step else near_far[1]))
        own = own.astype(jnp.float32) + other[:half].astype(jnp.float32)
        peer = (peer.astype(jnp.float32) + other[half:].astype(jnp.float32)).astype(jnp.bfloat16)
        ready = peer
        near_high, near_low = swap_near(peer[head:]), peer[:head]
        if step + 1 == steps:
            near_low = after(near_low, near_high)
        high = own[head:] + near_high.astype(jnp.float32)
        low = own[:head] + after(swap_near(near_low), high).astype(jnp.float32)
        high = swap_far(collapse(high).astype(jnp.bfloat16), middle)
        outputs.append((collapse(low) + high.astype(jnp.float32)).astype(jnp.bfloat16))
    return jnp.stack(outputs)


def solution(mesh):
    rows = P(None, ("groups", "expert"), None)
    weights = P("expert", None, None)
    return jax.shard_map(
        on_device,
        mesh=mesh,
        in_specs=(rows, rows, rows, P(), weights, weights, weights),
        out_specs=rows,
        check_vma=False,
    )
```

```python
import functools

import jax
import jax.numpy as jnp
from jax import lax
from jax.experimental import pallas as pl
from jax.experimental.pallas import tpu as pltpu
from jax.sharding import PartitionSpec as P

LANES = 128
MIB = 1 << 20


def in_vmem():
    return pl.BlockSpec(memory_space=pltpu.VMEM)


def message_kernel(states_ref, ids_ref, probs_ref, *message_refs):
    steps, tokens, width = states_ref.shape
    tail = message_refs[0].shape[1] - width
    half = tail // 2
    place = lax.broadcasted_iota(jnp.int32, (tail, tokens), 0)
    row = lax.broadcasted_iota(jnp.int32, (tokens, tokens), 0)
    column = lax.broadcasted_iota(jnp.int32, (tokens, tokens), 1)
    one = jnp.where(row == column, 1.0, 0.0).astype(jnp.bfloat16)
    for step in range(steps):
        probs = probs_ref[step]
        share = probs / jnp.sum(probs, axis=0, keepdims=True)
        ids = ids_ref[step]
        dense = jnp.zeros((tail, tokens), jnp.float32)
        for k in range(ids.shape[0]):
            dense += jnp.where(ids[k : k + 1] == place % half, share[k : k + 1], 0.0)
        high = dense.astype(jnp.bfloat16).astype(jnp.float32)
        terms = jnp.where(place < half, high, dense - high).astype(jnp.bfloat16)
        upright = lax.dot_general(one, terms, (((1,), (1,)), ((), ())), preferred_element_type=jnp.float32)
        upright = upright.astype(jnp.bfloat16)
        for message_ref, at in ((message_refs[0], step * tokens), (message_refs[step + 1], 0)):
            message_ref[at : at + tokens, :width] = states_ref[step]
            message_ref[at : at + tokens, width:] = upright


def make_messages(states, ids, probs, tail):
    steps, tokens, width = states.shape
    states, ids, probs = (pltpu.with_memory_space_constraint(x, pltpu.HBM) for x in (states, ids, probs))

    def whole(shape):
        return pl.BlockSpec(shape, lambda i: (0,) * len(shape))

    shapes = [(steps * tokens, width + tail)] + [(tokens, width + tail)] * steps
    return pl.pallas_call(
        message_kernel,
        grid=(1,),
        out_shape=[jax.ShapeDtypeStruct(shape, jnp.bfloat16) for shape in shapes],
        in_specs=[whole(x.shape) for x in (states, ids, probs)],
        out_specs=[whole(shape) for shape in shapes],
        compiler_params=pltpu.CompilerParams(vmem_limit_bytes=4 * MIB),
        name="messages",
    )(states, ids, probs)


def load_kernel(*refs):
    count = len(refs) // 3
    copies = [
        pltpu.make_async_copy(refs[i], refs[count + i], refs[2 * count + i]) for i in range(count)
    ]
    for copy in copies:
        copy.start()
    for copy in copies:
        copy.wait()


def load_weights(*arrays):
    arrays = [pltpu.with_memory_space_constraint(x, pltpu.HBM) for x in arrays]
    return pl.pallas_call(
        load_kernel,
        out_shape=[pltpu.VMEM(x.shape, x.dtype) for x in arrays],
        in_specs=[pl.BlockSpec(memory_space=pltpu.HBM)] * len(arrays),
        out_specs=[in_vmem()] * len(arrays),
        scratch_shapes=[pltpu.SemaphoreType.DMA(())] * len(arrays),
        cost_estimate=pl.CostEstimate(flops=0, bytes_accessed=0, transcendentals=0),
        compiler_params=pltpu.CompilerParams(vmem_limit_bytes=4 * MIB),
        name="load_weights",
    )(*arrays)


def expert_kernel(swapped, count, plan, flags_ref, gate_ref, up_ref, down_ref, *refs):
    *sources, own_ref, near_ref, low_ref, high_ref, rows, hidden = refs
    width, units = gate_ref.shape
    tail = rows.shape[1] - width
    owner = lax.axis_index("expert")
    slot = jnp.bitwise_xor(owner, flags_ref[owner]) if swapped else owner
    at = 0
    for source, low, high in plan:
        rows[at : at + high - low] = sources[source][low:high]
        at += high - low
    total = rows.shape[0]
    lane = lax.broadcasted_iota(jnp.int32, (total, tail), 1)
    terms = rows[:, width:].astype(jnp.float32)
    weight = jnp.sum(jnp.where(lane % (tail // 2) == slot, terms, 0.0), axis=1, keepdims=True)
    step = 256
    for at in range(0, units, step):
        gate = jnp.dot(rows[:, :width], gate_ref[:, at : at + step], preferred_element_type=jnp.float32)
        up = jnp.dot(rows[:, :width], up_ref[:, at : at + step], preferred_element_type=jnp.float32)
        value = gate / (1.0 + jnp.exp(-gate)) * up
        hidden[:, at : at + step] = (value * weight).astype(jnp.bfloat16)

    def columns(index, _):
        at = pl.ds(pl.multiple_of(index * 512, 512), 512)
        out = jnp.dot(hidden[...], down_ref[:, at], preferred_element_type=jnp.float32)
        out = out.astype(jnp.bfloat16)
        own_ref[:, at] = out[:count]
        near_ref[:, at] = out[count : 2 * count]
        for side in range(2):
            low, part = (2 + side) * count, slice(side * count // 2, (side + 1) * count // 2)
            low_ref[part, at] = out[low : low + count // 2]
            high_ref[part, at] = out[low + count // 2 : low + count]
        return 0

    lax.fori_loop(0, width // 512, columns, 0)


def run_expert(swapped, flags, weights, parts, plan):
    total = sum(high - low for _, low, high in plan)
    count = total // 4
    width, units = weights[0].shape
    weights = [pltpu.with_memory_space_constraint(w, pltpu.VMEM) for w in weights]
    return pl.pallas_call(
        functools.partial(expert_kernel, swapped, count, plan),
        out_shape=[jax.ShapeDtypeStruct((count, width), jnp.bfloat16)] * 4,
        in_specs=[pl.BlockSpec(memory_space=pltpu.SMEM)] + [in_vmem()] * (3 + len(parts)),
        out_specs=[in_vmem()] * 4,
        scratch_shapes=[
            pltpu.VMEM((total, parts[0].shape[1]), jnp.bfloat16),
            pltpu.VMEM((total, units), jnp.bfloat16),
        ],
        compiler_params=pltpu.CompilerParams(vmem_limit_bytes=16 * MIB),
        cost_estimate=pl.CostEstimate(
            flops=total * width * units * 6, bytes_accessed=4 * total * width, transcendentals=0
        ),
        name="expert",
    )(flags, *weights, *parts)


def add_kernel(first_ref, second_ref, sum_ref):
    sum_ref[...] = first_ref[...] + second_ref[...].astype(jnp.float32)


def add(first, second):
    return pl.pallas_call(
        add_kernel,
        out_shape=jax.ShapeDtypeStruct(first.shape, jnp.float32),
        in_specs=[in_vmem()] * 2,
        out_specs=in_vmem(),
        compiler_params=pltpu.CompilerParams(vmem_limit_bytes=4 * MIB),
        cost_estimate=pl.CostEstimate(flops=1 << 34, bytes_accessed=0, transcendentals=0),
        name="add",
    )(first, second)


def on_device(states, ids, probs, flags, w_gate, w_up, w_down):
    devices = lax.axis_size("expert")
    lines = devices // 4
    steps, tokens, width = states.shape

    def index(far, near, core):
        return far * 4 + near * 2 + core

    every = [(z, y, c) for z in range(lines) for y in range(2) for c in range(2)]

    def swap_core(x):
        return lax.ppermute(x, "expert", [(index(z, y, c), index(z, y, 1 - c)) for z, y, c in every])

    def swap_near(x):
        return lax.ppermute(x, "expert", [(index(z, y, c), index(z, 1 - y, c)) for z, y, c in every])

    def swap_far(x, by):
        return lax.ppermute(x, "expert", [(index(z, y, c), index(z ^ by, y, c)) for z, y, c in every])

    tail = 2 * devices
    tail = -(-tail // LANES) * LANES
    ids, probs = jnp.swapaxes(ids, 1, 2), jnp.swapaxes(probs, 1, 2)
    middle = lines // 2
    strides = [middle >> shift for shift in range(1, middle.bit_length())]
    head, half = middle * tokens, lines * tokens

    def grow(block):
        for by in strides:
            block = jnp.concatenate([block, swap_far(block, by)])
        return block

    def collapse(block):
        for by in strides[::-1]:
            keep = block.shape[0] // 2
            block = block[:keep] + swap_far(block[keep:].astype(jnp.bfloat16), by).astype(jnp.float32)
        return block

    def after(x, *events):
        return lax.optimization_barrier((x, events))[0]

    def of_step(x, step):
        return jnp.concatenate([x[at : at + tokens] for at in range(step * tokens, x.shape[0], steps * tokens)])

    w_gate, w_up, w_down = w_gate[0], w_up[0], w_down[0]
    message, *own_messages = make_messages(states, ids, probs, tail)
    near_message = swap_near(message)
    close = message
    received = []
    for by in strides:
        received.append(swap_far(close, by))
        close = jnp.concatenate([close, received[-1]])
    cross = swap_far(own_messages[0], middle)
    loaded = load_weights(w_gate, w_up)
    received, cross, near_message, loaded = lax.optimization_barrier((received, cross, near_message, loaded))
    close = jnp.concatenate([message, *received])
    far, near_far = [], []
    for step in range(steps):
        if step:
            far.append(grow(crossed))
            near_far.append(swap_near(jnp.concatenate([far[step], of_step(close, step)[tokens:]])))
            if step + 1 < steps:
                crossed = swap_far(after(own_messages[step + 1], crossed), middle)
        else:
            near = swap_near(of_step(close, step)[tokens:])
            if steps > 1:
                crossed = swap_far(after(own_messages[1], cross), middle)
            far.append(grow(cross))
            near_far.append(swap_near(far[0]))
            last = load_weights(after(w_down, far[0]))
            crossed, near_close, last = lax.optimization_barrier((crossed, near, last))
            loaded += last
    shared = jnp.concatenate([close, near_message, near_close])
    shared = [shared, swap_core(shared)]
    outputs, ready = [], far
    for step in range(steps):
        if step:
            rest = jnp.concatenate([far[step], near_far[step]])
            parts = [*shared, rest, swap_core(rest)]
        else:
            parts = [*shared, far[0], swap_core(after(far[0], crossed)), near_far[0], swap_core(near_far[0])]
        plan = []
        for core in range(2):
            for by in range(middle):
                at = (by * steps + step) * tokens
                plan.append((core, at, at + tokens))
            plan.append((2 + core, 0, head))
            at = (middle * steps + step) * tokens
            plan.append((core, at, at + tokens))
            at = 2 * head if step else (middle + 1) * steps * tokens
            plan.append((2 * (step > 0) + core, at, at + head - tokens))
            at = head if step else 0
            plan.append(((2 if step else 4) + core, at, at + head))
        own, peer, other_low, other_high = run_expert(step > 0, flags, loaded, after(parts, ready), tuple(plan))
        other_high = swap_core(other_high if step else after(other_high, near_far[1])).astype(jnp.float32)
        other_low = swap_core(after(other_low, near) if step else other_low)
        to_high = (peer[head:].astype(jnp.float32) + other_high[head:]).astype(jnp.bfloat16)
        other_low = after(other_low, to_high).astype(jnp.float32)
        to_low = (peer[:head].astype(jnp.float32) + other_low[head:]).astype(jnp.bfloat16)
        ready = to_high, to_low
        if step:
            near = after(near, to_high).astype(jnp.float32)
            high += near[head:]
            low += after(near[:head], high)
            high = swap_far(collapse(high).astype(jnp.bfloat16), middle)
            outputs.append((collapse(low), high))
        high = own[head:].astype(jnp.float32) + other_high[:head]
        low = own[:head].astype(jnp.float32) + other_low[:head]
        if step + 1 < steps:
            near = swap_near(jnp.concatenate([to_low, to_high]))
    near = swap_near(to_low)
    outputs = [low + after(high, near).astype(jnp.float32) for low, high in outputs]
    high = collapse(high + swap_near(to_high).astype(jnp.float32))
    low += after(near, high).astype(jnp.float32)
    first = add(low[:tokens], swap_far(high.astype(jnp.bfloat16), middle))
    outputs.append(collapse(jnp.concatenate([first, low[tokens:]])))
    return jnp.stack(outputs).astype(jnp.bfloat16)


def solution(mesh):
    rows = P(None, ("groups", "expert"), None)
    weights = P("expert", None, None)
    return jax.shard_map(
        on_device,
        mesh=mesh,
        in_specs=(rows, rows, rows, P(), weights, weights, weights),
        out_specs=rows,
        check_vma=False,
    )
```

```python
import functools

import jax
import jax.numpy as jnp
from jax import lax
from jax.experimental import pallas as pl
from jax.experimental.pallas import tpu as pltpu
from jax.sharding import PartitionSpec as P

LANES = 128
MIB = 1 << 20


def in_vmem():
    return pl.BlockSpec(memory_space=pltpu.VMEM)


def message_kernel(states_ref, ids_ref, probs_ref, *message_refs):
    steps, tokens, width = states_ref.shape
    tail = message_refs[0].shape[1] - width
    half = tail // 2
    place = lax.broadcasted_iota(jnp.int32, (tail, tokens), 0)
    row = lax.broadcasted_iota(jnp.int32, (tokens, tokens), 0)
    column = lax.broadcasted_iota(jnp.int32, (tokens, tokens), 1)
    one = jnp.where(row == column, 1.0, 0.0).astype(jnp.bfloat16)
    for step in range(steps):
        probs = probs_ref[step]
        share = probs / jnp.sum(probs, axis=0, keepdims=True)
        ids = ids_ref[step]
        dense = jnp.zeros((tail, tokens), jnp.float32)
        for k in range(ids.shape[0]):
            dense += jnp.where(ids[k : k + 1] == place % half, share[k : k + 1], 0.0)
        high = dense.astype(jnp.bfloat16).astype(jnp.float32)
        terms = jnp.where(place < half, high, dense - high).astype(jnp.bfloat16)
        upright = lax.dot_general(one, terms, (((1,), (1,)), ((), ())), preferred_element_type=jnp.float32)
        upright = upright.astype(jnp.bfloat16)
        message_refs[step][:, :width] = states_ref[step]
        message_refs[step][:, width:] = upright


def make_messages(states, ids, probs, tail):
    steps, tokens, width = states.shape
    states, ids, probs = (pltpu.with_memory_space_constraint(x, pltpu.HBM) for x in (states, ids, probs))

    def whole(shape):
        return pl.BlockSpec(shape, lambda i: (0,) * len(shape))

    shapes = [(tokens, width + tail)] * steps
    return pl.pallas_call(
        message_kernel,
        grid=(1,),
        out_shape=[jax.ShapeDtypeStruct(shape, jnp.bfloat16) for shape in shapes],
        in_specs=[whole(x.shape) for x in (states, ids, probs)],
        out_specs=[whole(shape) for shape in shapes],
        compiler_params=pltpu.CompilerParams(vmem_limit_bytes=4 * MIB),
        name="messages",
    )(states, ids, probs)


def load_kernel(*refs):
    count = len(refs) // 3
    copies = [
        pltpu.make_async_copy(refs[i], refs[count + i], refs[2 * count + i]) for i in range(count)
    ]
    for copy in copies:
        copy.start()
    for copy in copies:
        copy.wait()


def load_weights(*arrays):
    arrays = [pltpu.with_memory_space_constraint(x, pltpu.HBM) for x in arrays]
    return pl.pallas_call(
        load_kernel,
        out_shape=[pltpu.VMEM(x.shape, x.dtype) for x in arrays],
        in_specs=[pl.BlockSpec(memory_space=pltpu.HBM)] * len(arrays),
        out_specs=[in_vmem()] * len(arrays),
        scratch_shapes=[pltpu.SemaphoreType.DMA(())] * len(arrays),
        cost_estimate=pl.CostEstimate(flops=0, bytes_accessed=0, transcendentals=0),
        compiler_params=pltpu.CompilerParams(vmem_limit_bytes=4 * MIB),
        name="load_weights",
    )(*arrays)


def expert_kernel(swapped, count, plan, flags_ref, gate_ref, up_ref, down_ref, *refs):
    *sources, own_ref, near_ref, low_ref, high_ref, rows, hidden = refs
    width, units = gate_ref.shape
    tail = rows.shape[1] - width
    owner = lax.axis_index("expert")
    slot = jnp.bitwise_xor(owner, flags_ref[owner]) if swapped else owner
    at = 0
    for source, low, high in plan:
        rows[at : at + high - low] = sources[source][low:high]
        at += high - low
    total = rows.shape[0]
    lane = lax.broadcasted_iota(jnp.int32, (total, tail), 1)
    terms = rows[:, width:].astype(jnp.float32)
    weight = jnp.sum(jnp.where(lane % (tail // 2) == slot, terms, 0.0), axis=1, keepdims=True)
    step = 256
    for at in range(0, units, step):
        gate = jnp.dot(rows[:, :width], gate_ref[:, at : at + step], preferred_element_type=jnp.float32)
        up = jnp.dot(rows[:, :width], up_ref[:, at : at + step], preferred_element_type=jnp.float32)
        value = gate / (1.0 + jnp.exp(-gate)) * up
        hidden[:, at : at + step] = (value * weight).astype(jnp.bfloat16)

    def columns(index, _):
        at = pl.ds(pl.multiple_of(index * 512, 512), 512)
        out = jnp.dot(hidden[...], down_ref[:, at], preferred_element_type=jnp.float32)
        out = out.astype(jnp.bfloat16)
        own_ref[:, at] = out[:count]
        near_ref[:, at] = out[count : 2 * count]
        for side in range(2):
            low, part = (2 + side) * count, slice(side * count // 2, (side + 1) * count // 2)
            low_ref[part, at] = out[low : low + count // 2]
            high_ref[part, at] = out[low + count // 2 : low + count]
        return 0

    lax.fori_loop(0, width // 512, columns, 0)


def run_expert(swapped, flags, weights, parts, plan):
    total = sum(high - low for _, low, high in plan)
    count = total // 4
    width, units = weights[0].shape
    weights = [pltpu.with_memory_space_constraint(w, pltpu.VMEM) for w in weights]
    return pl.pallas_call(
        functools.partial(expert_kernel, swapped, count, plan),
        out_shape=[jax.ShapeDtypeStruct((count, width), jnp.bfloat16)] * 4,
        in_specs=[pl.BlockSpec(memory_space=pltpu.SMEM)] + [in_vmem()] * (3 + len(parts)),
        out_specs=[in_vmem()] * 4,
        scratch_shapes=[
            pltpu.VMEM((total, parts[0].shape[1]), jnp.bfloat16),
            pltpu.VMEM((total, units), jnp.bfloat16),
        ],
        compiler_params=pltpu.CompilerParams(vmem_limit_bytes=16 * MIB),
        cost_estimate=pl.CostEstimate(
            flops=total * width * units * 6, bytes_accessed=4 * total * width, transcendentals=0
        ),
        name="expert",
    )(flags, *weights, *parts)


def add_kernel(first_ref, second_ref, sum_ref):
    sum_ref[...] = first_ref[...] + second_ref[...].astype(jnp.float32)


def add(first, second):
    return pl.pallas_call(
        add_kernel,
        out_shape=jax.ShapeDtypeStruct(first.shape, jnp.float32),
        in_specs=[in_vmem()] * 2,
        out_specs=in_vmem(),
        compiler_params=pltpu.CompilerParams(vmem_limit_bytes=4 * MIB),
        cost_estimate=pl.CostEstimate(flops=1 << 34, bytes_accessed=0, transcendentals=0),
        name="add",
    )(first, second)


def on_device(states, ids, probs, flags, w_gate, w_up, w_down):
    devices = lax.axis_size("expert")
    lines = devices // 4
    steps, tokens, width = states.shape

    def index(far, near, core):
        return far * 4 + near * 2 + core

    every = [(z, y, c) for z in range(lines) for y in range(2) for c in range(2)]

    def swap_core(x):
        return lax.ppermute(x, "expert", [(index(z, y, c), index(z, y, 1 - c)) for z, y, c in every])

    def swap_near(x):
        return lax.ppermute(x, "expert", [(index(z, y, c), index(z, 1 - y, c)) for z, y, c in every])

    def swap_far(x, by):
        return lax.ppermute(x, "expert", [(index(z, y, c), index(z ^ by, y, c)) for z, y, c in every])

    tail = 2 * devices
    tail = -(-tail // LANES) * LANES
    ids, probs = jnp.swapaxes(ids, 1, 2), jnp.swapaxes(probs, 1, 2)
    middle = lines // 2
    strides = [middle >> shift for shift in range(1, middle.bit_length())]
    head, half = middle * tokens, lines * tokens

    def grow(block, strides):
        for by in strides:
            block = jnp.concatenate([block, swap_far(block, by)])
        return block

    def places(strides):
        found = [0]
        for by in strides:
            found += [place ^ by for place in found]
        return found

    def collapse(block):
        for by in strides[::-1]:
            keep = block.shape[0] // 2
            block = block[:keep] + swap_far(block[keep:].astype(jnp.bfloat16), by).astype(jnp.float32)
        return block

    def after(x, *events):
        return lax.optimization_barrier((x, events))[0]

    w_gate, w_up, w_down = w_gate[0], w_up[0], w_down[0]
    messages = make_messages(states, ids, probs, tail)
    far = swap_far(messages[0], middle)
    close = [messages[0], *[swap_far(messages[0], by) for by in places(strides)[1:]]]
    near_close = [swap_near(messages[0])]
    loaded = load_weights(w_gate, w_up)
    far, close, near_close, loaded = lax.optimization_barrier((far, close, near_close, loaded))
    others = close[1:]
    near_close += [swap_near(block) for block in others]
    crossed = [swap_far(after(message, far), middle) for message in messages[1:]]
    far = grow(far, strides)
    near_far = swap_near(far)
    last = load_weights(after(w_down, far))
    near_own = [swap_near(after(message, others)) for message in messages[1:]]
    crossed, near_close, near_own, last = lax.optimization_barrier((crossed, near_close, near_own, last))
    loaded += last
    line = jnp.concatenate([*close, far, *near_close])
    sources = [[line, swap_core(line), near_far, swap_core(near_far)]]
    wanted = places(strides)
    wanted += [middle ^ place for place in wanted]
    found = places([middle] + strides)
    for message, block, near in zip(messages[1:], crossed, near_own):
        line = grow(jnp.concatenate([message, block]), strides)
        near_line = swap_near(line[tokens:])
        line = jnp.concatenate([line, near])
        sources.append([line, swap_core(line), near_line, swap_core(near_line)])
    outputs, ready = [], [source[0] for source in sources]
    for step in range(steps):
        plan = []
        for core in range(2):
            if step:
                at = [found.index(place) * tokens for place in wanted]
                plan += [(core, low, low + tokens) for low in at] + [(core, half, half + tokens)]
                plan += [(2 + core, low - tokens, low) for low in at[1:]]
            else:
                plan += [(core, 0, half + head), (2 + core, 0, head)]
        parts = sources[step]
        own, peer, other_low, other_high = run_expert(step > 0, flags, loaded, after(parts, ready), tuple(plan))
        other_high = swap_core(other_high if step else after(other_high, sources[1][2]))
        if step:
            other_high = after(other_high, near)
        other_high = other_high.astype(jnp.float32)
        other_low = swap_core(after(other_low, near if step else sources[1][2]))
        to_high = (peer[head:].astype(jnp.float32) + other_high[head:]).astype(jnp.bfloat16)
        other_low = after(other_low, to_high).astype(jnp.float32)
        to_low = (peer[:head].astype(jnp.float32) + other_low[head:]).astype(jnp.bfloat16)
        ready = to_high, to_low
        if step:
            near = after(near, to_high).astype(jnp.float32)
            high += near[head:]
            low += after(near[:head], high)
            high = swap_far(collapse(high).astype(jnp.bfloat16), middle)
            outputs.append((collapse(low), high))
        high = own[head:].astype(jnp.float32) + other_high[:head]
        low = own[:head].astype(jnp.float32) + other_low[:head]
        if step + 1 < steps:
            near = swap_near(jnp.concatenate([to_low, to_high]))
    near = swap_near(to_low)
    outputs = [low + after(high, near).astype(jnp.float32) for low, high in outputs]
    high = collapse(high + swap_near(to_high).astype(jnp.float32))
    low += after(near, high).astype(jnp.float32)
    first = add(low[:tokens], swap_far(high.astype(jnp.bfloat16), middle))
    outputs.append(collapse(jnp.concatenate([first, low[tokens:]])))
    return jnp.stack(outputs).astype(jnp.bfloat16)


def solution(mesh):
    rows = P(None, ("groups", "expert"), None)
    weights = P("expert", None, None)
    return jax.shard_map(
        on_device,
        mesh=mesh,
        in_specs=(rows, rows, rows, P(), weights, weights, weights),
        out_specs=rows,
        check_vma=False,
    )
```

```python
import functools

import jax
import jax.numpy as jnp
from jax import lax
from jax.experimental import pallas as pl
from jax.experimental.pallas import tpu as pltpu
from jax.sharding import PartitionSpec as P

LANES = 128
MIB = 1 << 20


def in_vmem():
    return pl.BlockSpec(memory_space=pltpu.VMEM)


def message_kernel(states_ref, ids_ref, probs_ref, *message_refs):
    steps, tokens, width = states_ref.shape
    tail = message_refs[0].shape[1] - width
    half = tail // 2
    place = lax.broadcasted_iota(jnp.int32, (tail, tokens), 0)
    row = lax.broadcasted_iota(jnp.int32, (tokens, tokens), 0)
    column = lax.broadcasted_iota(jnp.int32, (tokens, tokens), 1)
    one = jnp.where(row == column, 1.0, 0.0).astype(jnp.bfloat16)
    for step in range(steps):
        probs = probs_ref[step]
        share = probs / jnp.sum(probs, axis=0, keepdims=True)
        ids = ids_ref[step]
        dense = jnp.zeros((tail, tokens), jnp.float32)
        for k in range(ids.shape[0]):
            dense += jnp.where(ids[k : k + 1] == place % half, share[k : k + 1], 0.0)
        high = dense.astype(jnp.bfloat16).astype(jnp.float32)
        terms = jnp.where(place < half, high, dense - high).astype(jnp.bfloat16)
        upright = lax.dot_general(one, terms, (((1,), (1,)), ((), ())), preferred_element_type=jnp.float32)
        upright = upright.astype(jnp.bfloat16)
        message_refs[step][:, :width] = states_ref[step]
        message_refs[step][:, width:] = upright


def make_messages(states, ids, probs, tail):
    steps, tokens, width = states.shape
    states, ids, probs = (pltpu.with_memory_space_constraint(x, pltpu.HBM) for x in (states, ids, probs))

    def whole(shape):
        return pl.BlockSpec(shape, lambda i: (0,) * len(shape))

    shapes = [(tokens, width + tail)] * steps
    return pl.pallas_call(
        message_kernel,
        grid=(1,),
        out_shape=[jax.ShapeDtypeStruct(shape, jnp.bfloat16) for shape in shapes],
        in_specs=[whole(x.shape) for x in (states, ids, probs)],
        out_specs=[whole(shape) for shape in shapes],
        compiler_params=pltpu.CompilerParams(vmem_limit_bytes=4 * MIB),
        name="messages",
    )(states, ids, probs)


def load_kernel(*refs):
    count = len(refs) // 3
    copies = [
        pltpu.make_async_copy(refs[i], refs[count + i], refs[2 * count + i]) for i in range(count)
    ]
    for copy in copies:
        copy.start()
    for copy in copies:
        copy.wait()


def load_weights(*arrays):
    arrays = [pltpu.with_memory_space_constraint(x, pltpu.HBM) for x in arrays]
    return pl.pallas_call(
        load_kernel,
        out_shape=[pltpu.VMEM(x.shape, x.dtype) for x in arrays],
        in_specs=[pl.BlockSpec(memory_space=pltpu.HBM)] * len(arrays),
        out_specs=[in_vmem()] * len(arrays),
        scratch_shapes=[pltpu.SemaphoreType.DMA(())] * len(arrays),
        cost_estimate=pl.CostEstimate(flops=0, bytes_accessed=0, transcendentals=0),
        compiler_params=pltpu.CompilerParams(vmem_limit_bytes=4 * MIB),
        name="load_weights",
    )(*arrays)


def expert_kernel(swapped, count, plan, flags_ref, gate_ref, up_ref, down_ref, *refs):
    *sources, own_ref, near_ref, low_ref, high_ref, rows, hidden = refs
    width, units = gate_ref.shape
    tail = rows.shape[1] - width
    owner = lax.axis_index("expert")
    slot = jnp.bitwise_xor(owner, flags_ref[owner]) if swapped else owner
    at = 0
    for source, low, high in plan:
        rows[at : at + high - low] = sources[source][low:high]
        at += high - low
    total = rows.shape[0]
    lane = lax.broadcasted_iota(jnp.int32, (total, tail), 1)
    terms = rows[:, width:].astype(jnp.float32)
    weight = jnp.sum(jnp.where(lane % (tail // 2) == slot, terms, 0.0), axis=1, keepdims=True)
    step = 256
    for at in range(0, units, step):
        gate = jnp.dot(rows[:, :width], gate_ref[:, at : at + step], preferred_element_type=jnp.float32)
        up = jnp.dot(rows[:, :width], up_ref[:, at : at + step], preferred_element_type=jnp.float32)
        value = gate / (1.0 + jnp.exp(-gate)) * up
        hidden[:, at : at + step] = (value * weight).astype(jnp.bfloat16)

    for at in range(0, width, 512):
        part = slice(at, at + 512)
        out = jnp.dot(hidden[...], down_ref[:, part], preferred_element_type=jnp.float32)
        out = out.astype(jnp.bfloat16)
        own_ref[:, part] = out[:count]
        near_ref[:, part] = out[count : 2 * count]
        for side in range(2):
            low, rows_of = (2 + side) * count, slice(side * count // 2, (side + 1) * count // 2)
            low_ref[rows_of, part] = out[low : low + count // 2]
            high_ref[rows_of, part] = out[low + count // 2 : low + count]


def run_expert(swapped, flags, weights, parts, plan):
    total = sum(high - low for _, low, high in plan)
    count = total // 4
    width, units = weights[0].shape
    weights = [pltpu.with_memory_space_constraint(w, pltpu.VMEM) for w in weights]
    return pl.pallas_call(
        functools.partial(expert_kernel, swapped, count, plan),
        out_shape=[jax.ShapeDtypeStruct((count, width), jnp.bfloat16)] * 4,
        in_specs=[pl.BlockSpec(memory_space=pltpu.SMEM)] + [in_vmem()] * (3 + len(parts)),
        out_specs=[in_vmem()] * 4,
        scratch_shapes=[
            pltpu.VMEM((total, parts[0].shape[1]), jnp.bfloat16),
            pltpu.VMEM((total, units), jnp.bfloat16),
        ],
        compiler_params=pltpu.CompilerParams(vmem_limit_bytes=16 * MIB),
        cost_estimate=pl.CostEstimate(
            flops=total * width * units * 6, bytes_accessed=4 * total * width, transcendentals=0
        ),
        name="expert",
    )(flags, *weights, *parts)


def add_kernel(first_ref, second_ref, sum_ref):
    sum_ref[...] = first_ref[...] + second_ref[...].astype(jnp.float32)


def add(first, second):
    return pl.pallas_call(
        add_kernel,
        out_shape=jax.ShapeDtypeStruct(first.shape, jnp.float32),
        in_specs=[in_vmem()] * 2,
        out_specs=in_vmem(),
        compiler_params=pltpu.CompilerParams(vmem_limit_bytes=4 * MIB),
        cost_estimate=pl.CostEstimate(flops=1 << 34, bytes_accessed=0, transcendentals=0),
        name="add",
    )(first, second)


def on_device(states, ids, probs, flags, w_gate, w_up, w_down):
    devices = lax.axis_size("expert")
    lines = devices // 4
    steps, tokens, width = states.shape

    def index(far, near, core):
        return far * 4 + near * 2 + core

    every = [(z, y, c) for z in range(lines) for y in range(2) for c in range(2)]

    def swap_core(x):
        return lax.ppermute(x, "expert", [(index(z, y, c), index(z, y, 1 - c)) for z, y, c in every])

    def swap_near(x):
        return lax.ppermute(x, "expert", [(index(z, y, c), index(z, 1 - y, c)) for z, y, c in every])

    def swap_far(x, by):
        return lax.ppermute(x, "expert", [(index(z, y, c), index(z ^ by, y, c)) for z, y, c in every])

    tail = 2 * devices
    tail = -(-tail // LANES) * LANES
    ids, probs = jnp.swapaxes(ids, 1, 2), jnp.swapaxes(probs, 1, 2)
    middle = lines // 2
    strides = [middle >> shift for shift in range(1, middle.bit_length())]
    head, half = middle * tokens, lines * tokens

    def grow(block, strides):
        for by in strides:
            block = jnp.concatenate([block, swap_far(block, by)])
        return block

    def places(strides):
        found = [0]
        for by in strides:
            found += [place ^ by for place in found]
        return found

    def collapse(block):
        for by in strides[::-1]:
            keep = block.shape[0] // 2
            block = block[:keep] + swap_far(block[keep:].astype(jnp.bfloat16), by).astype(jnp.float32)
        return block

    def after(x, *events):
        return lax.optimization_barrier((x, events))[0]

    w_gate, w_up, w_down = w_gate[0], w_up[0], w_down[0]
    messages = make_messages(states, ids, probs, tail)
    far = swap_far(messages[0], middle)
    close = [messages[0], *[swap_far(messages[0], by) for by in places(strides)[1:]]]
    near_close = [swap_near(messages[0])]
    loaded = load_weights(w_gate, w_up)
    loaded, near_close, close, far = lax.optimization_barrier((loaded, near_close, close, far))
    others = close[1:]
    near_close += [swap_near(block) for block in others]
    crossed = [swap_far(after(message, far), middle) for message in messages[1:]]
    far = grow(far, strides)
    near_far = swap_near(far)
    last = load_weights(after(w_down, far))
    near_own = [swap_near(after(message, others)) for message in messages[1:]]
    crossed, near_close, near_own, last = lax.optimization_barrier((crossed, near_close, near_own, last))
    loaded += last
    line = jnp.concatenate([*close, far, *near_close])
    sources = [[line, swap_core(line), near_far, swap_core(near_far)]]
    wanted = places(strides)
    wanted += [middle ^ place for place in wanted]
    found = places([middle] + strides)
    for message, block, near in zip(messages[1:], crossed, near_own):
        line = after(grow(jnp.concatenate([message, block]), strides), near_far)
        near_line = swap_near(line[tokens:])
        line = jnp.concatenate([line, near])
        sources.append([line, swap_core(line), near_line, swap_core(near_line)])
    outputs, ready = [], [source[0] for source in sources]
    for step in range(steps):
        plan = []
        for core in range(2):
            if step:
                at = [found.index(place) * tokens for place in wanted]
                plan += [(core, low, low + tokens) for low in at] + [(core, half, half + tokens)]
                plan += [(2 + core, low - tokens, low) for low in at[1:]]
            else:
                plan += [(core, 0, half + head), (2 + core, 0, head)]
        parts = sources[step]
        own, peer, other_low, other_high = run_expert(step > 0, flags, loaded, after(parts, ready), tuple(plan))
        other_high = swap_core(other_high if step else after(other_high, sources[1][1:3]))
        if step:
            other_high = after(other_high, near)
        other_high = other_high.astype(jnp.float32)
        other_low = swap_core(after(other_low, near if step else sources[1][2]))
        to_high = (peer[head:].astype(jnp.float32) + other_high[head:]).astype(jnp.bfloat16)
        other_low = after(other_low, to_high).astype(jnp.float32)
        to_low = (peer[:head].astype(jnp.float32) + other_low[head:]).astype(jnp.bfloat16)
        ready = to_high, to_low
        if step:
            near = after(near, to_high).astype(jnp.float32)
            high = collapse(high + near[head:])
            low += after(near[:head], high)
            high = swap_far(high.astype(jnp.bfloat16), middle)
            outputs.append((collapse(low), high))
        high = own[head:].astype(jnp.float32) + other_high[:head]
        low = own[:head].astype(jnp.float32) + other_low[:head]
        if step + 1 < steps:
            near = swap_near(jnp.concatenate([to_low, to_high]))
    near = swap_near(to_low)
    outputs = [low + after(high, near).astype(jnp.float32) for low, high in outputs]
    high = collapse(high + swap_near(to_high).astype(jnp.float32))
    low += after(near, high).astype(jnp.float32)
    first = add(low[:tokens], swap_far(high.astype(jnp.bfloat16), middle))
    outputs.append(collapse(jnp.concatenate([first, low[tokens:]])))
    return jnp.stack(outputs).astype(jnp.bfloat16)


def solution(mesh):
    rows = P(None, ("groups", "expert"), None)
    weights = P("expert", None, None)
    return jax.shard_map(
        on_device,
        mesh=mesh,
        in_specs=(rows, rows, rows, P(), weights, weights, weights),
        out_specs=rows,
        check_vma=False,
    )
```

```python
import functools

import jax
import jax.numpy as jnp
from jax import lax
from jax.experimental import pallas as pl
from jax.experimental.pallas import tpu as pltpu
from jax.sharding import PartitionSpec as P

LANES = 128
MIB = 1 << 20


def in_vmem():
    return pl.BlockSpec(memory_space=pltpu.VMEM)


def message_kernel(states_ref, ids_ref, probs_ref, *message_refs):
    steps, tokens, width = states_ref.shape
    tail = message_refs[0].shape[1] - width
    half = tail // 2
    place = lax.broadcasted_iota(jnp.int32, (tail, tokens), 0)
    row = lax.broadcasted_iota(jnp.int32, (tokens, tokens), 0)
    column = lax.broadcasted_iota(jnp.int32, (tokens, tokens), 1)
    one = jnp.where(row == column, 1.0, 0.0).astype(jnp.bfloat16)
    for step in range(steps):
        probs = probs_ref[step]
        share = probs / jnp.sum(probs, axis=0, keepdims=True)
        ids = ids_ref[step]
        dense = jnp.zeros((tail, tokens), jnp.float32)
        for k in range(ids.shape[0]):
            dense += jnp.where(ids[k : k + 1] == place % half, share[k : k + 1], 0.0)
        high = dense.astype(jnp.bfloat16).astype(jnp.float32)
        terms = jnp.where(place < half, high, dense - high).astype(jnp.bfloat16)
        upright = lax.dot_general(one, terms, (((1,), (1,)), ((), ())), preferred_element_type=jnp.float32)
        upright = upright.astype(jnp.bfloat16)
        message_refs[step][:, :width] = states_ref[step]
        message_refs[step][:, width:] = upright


def make_messages(states, ids, probs, tail):
    steps, tokens, width = states.shape
    states, ids, probs = (pltpu.with_memory_space_constraint(x, pltpu.HBM) for x in (states, ids, probs))

    def whole(shape):
        return pl.BlockSpec(shape, lambda i: (0,) * len(shape))

    shapes = [(tokens, width + tail)] * steps
    return pl.pallas_call(
        message_kernel,
        grid=(1,),
        out_shape=[jax.ShapeDtypeStruct(shape, jnp.bfloat16) for shape in shapes],
        in_specs=[whole(x.shape) for x in (states, ids, probs)],
        out_specs=[whole(shape) for shape in shapes],
        compiler_params=pltpu.CompilerParams(vmem_limit_bytes=4 * MIB),
        name="messages",
    )(states, ids, probs)


def load_kernel(*refs):
    count = len(refs) // 3
    copies = [
        pltpu.make_async_copy(refs[i], refs[count + i], refs[2 * count + i]) for i in range(count)
    ]
    for copy in copies:
        copy.start()
    for copy in copies:
        copy.wait()


def load_weights(*arrays):
    arrays = [pltpu.with_memory_space_constraint(x, pltpu.HBM) for x in arrays]
    return pl.pallas_call(
        load_kernel,
        out_shape=[pltpu.VMEM(x.shape, x.dtype) for x in arrays],
        in_specs=[pl.BlockSpec(memory_space=pltpu.HBM)] * len(arrays),
        out_specs=[in_vmem()] * len(arrays),
        scratch_shapes=[pltpu.SemaphoreType.DMA(())] * len(arrays),
        cost_estimate=pl.CostEstimate(flops=0, bytes_accessed=0, transcendentals=0),
        compiler_params=pltpu.CompilerParams(vmem_limit_bytes=4 * MIB),
        name="load_weights",
    )(*arrays)


def expert_kernel(swapped, count, plan, flags_ref, gate_ref, up_ref, down_ref, *refs):
    *sources, own_ref, near_ref, low_ref, high_ref, rows, hidden = refs
    width, units = gate_ref.shape
    tail = rows.shape[1] - width
    owner = lax.axis_index("expert")
    slot = jnp.bitwise_xor(owner, flags_ref[owner]) if swapped else owner
    at = 0
    for source, low, high in plan:
        rows[at : at + high - low] = sources[source][low:high]
        at += high - low
    total = rows.shape[0]
    lane = lax.broadcasted_iota(jnp.int32, (total, tail), 1)
    terms = rows[:, width:].astype(jnp.float32)
    weight = jnp.sum(jnp.where(lane % (tail // 2) == slot, terms, 0.0), axis=1, keepdims=True)
    step = 256
    for at in range(0, units, step):
        gate = jnp.dot(rows[:, :width], gate_ref[:, at : at + step], preferred_element_type=jnp.float32)
        up = jnp.dot(rows[:, :width], up_ref[:, at : at + step], preferred_element_type=jnp.float32)
        value = gate / (1.0 + jnp.exp(-gate)) * up
        hidden[:, at : at + step] = (value * weight).astype(jnp.bfloat16)

    for at in range(0, width, 512):
        part = slice(at, at + 512)
        out = jnp.dot(hidden[...], down_ref[:, part], preferred_element_type=jnp.float32)
        out = out.astype(jnp.bfloat16)
        own_ref[:, part] = out[:count]
        near_ref[:, part] = out[count : 2 * count]
        for side in range(2):
            low, rows_of = (2 + side) * count, slice(side * count // 2, (side + 1) * count // 2)
            low_ref[rows_of, part] = out[low : low + count // 2]
            high_ref[rows_of, part] = out[low + count // 2 : low + count]


def run_expert(swapped, flags, weights, parts, plan):
    total = sum(high - low for _, low, high in plan)
    count = total // 4
    width, units = weights[0].shape
    weights = [pltpu.with_memory_space_constraint(w, pltpu.VMEM) for w in weights]
    return pl.pallas_call(
        functools.partial(expert_kernel, swapped, count, plan),
        out_shape=[jax.ShapeDtypeStruct((count, width), jnp.bfloat16)] * 4,
        in_specs=[pl.BlockSpec(memory_space=pltpu.SMEM)] + [in_vmem()] * (3 + len(parts)),
        out_specs=[in_vmem()] * 4,
        scratch_shapes=[
            pltpu.VMEM((total, parts[0].shape[1]), jnp.bfloat16),
            pltpu.VMEM((total, units), jnp.bfloat16),
        ],
        compiler_params=pltpu.CompilerParams(vmem_limit_bytes=16 * MIB),
        cost_estimate=pl.CostEstimate(
            flops=total * width * units * 6, bytes_accessed=4 * total * width, transcendentals=0
        ),
        name="expert",
    )(flags, *weights, *parts)


def add_kernel(first_ref, second_ref, sum_ref):
    sum_ref[...] = first_ref[...] + second_ref[...].astype(jnp.float32)


def add(first, second):
    return pl.pallas_call(
        add_kernel,
        out_shape=jax.ShapeDtypeStruct(first.shape, jnp.float32),
        in_specs=[in_vmem()] * 2,
        out_specs=in_vmem(),
        compiler_params=pltpu.CompilerParams(vmem_limit_bytes=4 * MIB),
        cost_estimate=pl.CostEstimate(flops=1 << 34, bytes_accessed=0, transcendentals=0),
        name="add",
    )(first, second)


def on_device(states, ids, probs, flags, w_gate, w_up, w_down):
    devices = lax.axis_size("expert")
    lines = devices // 4
    steps, tokens, width = states.shape

    def index(far, near, core):
        return far * 4 + near * 2 + core

    every = [(z, y, c) for z in range(lines) for y in range(2) for c in range(2)]

    def swap_core(x):
        return lax.ppermute(x, "expert", [(index(z, y, c), index(z, y, 1 - c)) for z, y, c in every])

    def swap_near(x):
        return lax.ppermute(x, "expert", [(index(z, y, c), index(z, 1 - y, c)) for z, y, c in every])

    def swap_far(x, by):
        return lax.ppermute(x, "expert", [(index(z, y, c), index(z ^ by, y, c)) for z, y, c in every])

    tail = 2 * devices
    tail = -(-tail // LANES) * LANES
    ids, probs = jnp.swapaxes(ids, 1, 2), jnp.swapaxes(probs, 1, 2)
    middle = lines // 2
    strides = [middle >> shift for shift in range(1, middle.bit_length())]
    head, half = middle * tokens, lines * tokens

    def grow(block, strides):
        for by in strides:
            block = jnp.concatenate([block, swap_far(block, by)])
        return block

    def places(strides):
        found = [0]
        for by in strides:
            found += [place ^ by for place in found]
        return found

    def collapse(block):
        for by in strides[::-1]:
            keep = block.shape[0] // 2
            block = block[:keep] + swap_far(block[keep:].astype(jnp.bfloat16), by).astype(jnp.float32)
        return block

    def after(x, *events):
        return lax.optimization_barrier((x, events))[0]

    w_gate, w_up, w_down = w_gate[0], w_up[0], w_down[0]
    messages = make_messages(states, ids, probs, tail)
    far = swap_far(messages[0], middle)
    others = [swap_far(messages[0], by) for by in places(strides)[1:]]
    near_own = [swap_near(message) for message in messages]
    loaded = load_weights(w_gate, w_up)
    loaded, near_own, others, far = lax.optimization_barrier((loaded, near_own, others, far))
    near_close = [swap_near(block) for block in others]
    crossed = [swap_far(after(message, far), middle) for message in messages[1:]]
    far = grow(far, strides)
    near_far = swap_near(far)
    last = load_weights(after(w_down, far))
    last, near_close, crossed = lax.optimization_barrier((last, near_close, crossed))
    loaded += last
    line = jnp.concatenate([messages[0], *others, far, near_own[0], *near_close])
    sources = [[line, swap_core(line), near_far, swap_core(near_far)]]
    wanted = places(strides)
    wanted += [middle ^ place for place in wanted]
    found = places([middle] + strides)
    for step in range(1, steps):
        block = crossed[step - 1]
        near_block = swap_near(block)
        line = jnp.concatenate([messages[step], block])
        rest = []
        for by in strides:
            rest.append(after(swap_far(line, by), sources[0][3]))
            line = jnp.concatenate([line, rest[-1]])
        near_rest = swap_near(jnp.concatenate(rest))
        line = jnp.concatenate([messages[step], block, *rest, near_own[step], near_block])
        sources.append([line, swap_core(line), near_rest])
    outputs, ready = [], [source[0] for source in sources]
    for step in range(steps):
        plan = []
        for core in range(2):
            if step:
                at = [found.index(place) * tokens for place in wanted]
                plan += [(core, row, row + tokens) for row in at]
                for row in at:
                    early = row < 2 * tokens
                    row += half if early else -2 * tokens
                    plan.append((core if early else 2 + core, row, row + tokens))
            else:
                plan += [(core, 0, half + head), (2 + core, 0, head)]
        parts = sources[step]
        if step:
            parts = [*parts, swap_core(after(parts[2], ready))]
        own, peer, other_low, other_high = run_expert(step > 0, flags, loaded, after(parts, ready), tuple(plan))
        other_high = swap_core(other_high if step else after(other_high, sources[1][1:3]))
        if step:
            other_high = after(other_high, near)
        other_high = other_high.astype(jnp.float32)
        other_low = swap_core(after(other_low, near if step else sources[1][2]))
        to_high = (peer[head:].astype(jnp.float32) + other_high[head:]).astype(jnp.bfloat16)
        other_low = after(other_low, to_high).astype(jnp.float32)
        to_low = (peer[:head].astype(jnp.float32) + other_low[head:]).astype(jnp.bfloat16)
        ready = to_high, to_low
        if step:
            near = after(near, to_high).astype(jnp.float32)
            high = collapse(high + near[head:])
            low += after(near[:head], high)
            high = swap_far(high.astype(jnp.bfloat16), middle)
            outputs.append((collapse(low), high))
        high = own[head:].astype(jnp.float32) + other_high[:head]
        low = own[:head].astype(jnp.float32) + other_low[:head]
        if step + 1 < steps:
            near = swap_near(jnp.concatenate([to_low, to_high]))
    near = swap_near(to_low)
    outputs = [low + after(high, near).astype(jnp.float32) for low, high in outputs]
    high = collapse(high + swap_near(to_high).astype(jnp.float32))
    low += after(near, high).astype(jnp.float32)
    first = add(low[:tokens], swap_far(high.astype(jnp.bfloat16), middle))
    outputs.append(collapse(jnp.concatenate([first, low[tokens:]])))
    return jnp.stack(outputs).astype(jnp.bfloat16)


def solution(mesh):
    rows = P(None, ("groups", "expert"), None)
    weights = P("expert", None, None)
    return jax.shard_map(
        on_device,
        mesh=mesh,
        in_specs=(rows, rows, rows, P(), weights, weights, weights),
        out_specs=rows,
        check_vma=False,
    )
```

```python
import functools

import jax
import jax.numpy as jnp
from jax import lax
from jax.experimental import pallas as pl
from jax.experimental.pallas import tpu as pltpu
from jax.sharding import PartitionSpec as P

LANES = 128
MIB = 1 << 20


def in_vmem():
    return pl.BlockSpec(memory_space=pltpu.VMEM)


def message_kernel(states_ref, ids_ref, probs_ref, *message_refs):
    steps, tokens, width = states_ref.shape
    tail = message_refs[0].shape[1] - width
    half = tail // 2
    place = lax.broadcasted_iota(jnp.int32, (tail, tokens), 0)
    row = lax.broadcasted_iota(jnp.int32, (tokens, tokens), 0)
    column = lax.broadcasted_iota(jnp.int32, (tokens, tokens), 1)
    one = jnp.where(row == column, 1.0, 0.0).astype(jnp.bfloat16)
    for step in range(steps):
        probs = probs_ref[step]
        share = probs / jnp.sum(probs, axis=0, keepdims=True)
        ids = ids_ref[step]
        dense = jnp.zeros((tail, tokens), jnp.float32)
        for k in range(ids.shape[0]):
            dense += jnp.where(ids[k : k + 1] == place % half, share[k : k + 1], 0.0)
        high = dense.astype(jnp.bfloat16).astype(jnp.float32)
        terms = jnp.where(place < half, high, dense - high).astype(jnp.bfloat16)
        upright = lax.dot_general(one, terms, (((1,), (1,)), ((), ())), preferred_element_type=jnp.float32)
        upright = upright.astype(jnp.bfloat16)
        message_refs[step][:, :width] = states_ref[step]
        message_refs[step][:, width:] = upright


def make_messages(states, ids, probs, tail):
    steps, tokens, width = states.shape
    states, ids, probs = (pltpu.with_memory_space_constraint(x, pltpu.HBM) for x in (states, ids, probs))

    def whole(shape):
        return pl.BlockSpec(shape, lambda i: (0,) * len(shape))

    shapes = [(tokens, width + tail)] * steps
    return pl.pallas_call(
        message_kernel,
        grid=(1,),
        out_shape=[jax.ShapeDtypeStruct(shape, jnp.bfloat16) for shape in shapes],
        in_specs=[whole(x.shape) for x in (states, ids, probs)],
        out_specs=[whole(shape) for shape in shapes],
        compiler_params=pltpu.CompilerParams(vmem_limit_bytes=4 * MIB),
        name="messages",
    )(states, ids, probs)


def load_kernel(*refs):
    count = len(refs) // 3
    copies = [
        pltpu.make_async_copy(refs[i], refs[count + i], refs[2 * count + i]) for i in range(count)
    ]
    for copy in copies:
        copy.start()
    for copy in copies:
        copy.wait()


def load_weights(*arrays):
    arrays = [pltpu.with_memory_space_constraint(x, pltpu.HBM) for x in arrays]
    return pl.pallas_call(
        load_kernel,
        out_shape=[pltpu.VMEM(x.shape, x.dtype) for x in arrays],
        in_specs=[pl.BlockSpec(memory_space=pltpu.HBM)] * len(arrays),
        out_specs=[in_vmem()] * len(arrays),
        scratch_shapes=[pltpu.SemaphoreType.DMA(())] * len(arrays),
        cost_estimate=pl.CostEstimate(flops=0, bytes_accessed=0, transcendentals=0),
        compiler_params=pltpu.CompilerParams(vmem_limit_bytes=4 * MIB),
        name="load_weights",
    )(*arrays)


def expert_kernel(swapped, count, plan, flags_ref, gate_ref, up_ref, down_ref, *refs):
    *sources, own_ref, near_ref, low_ref, high_ref, rows, hidden = refs
    width, units = gate_ref.shape
    tail = rows.shape[1] - width
    owner = lax.axis_index("expert")
    slot = jnp.bitwise_xor(owner, flags_ref[owner]) if swapped else owner
    at = 0
    for source, low, high in plan:
        rows[at : at + high - low] = sources[source][low:high]
        at += high - low
    total = rows.shape[0]
    lane = lax.broadcasted_iota(jnp.int32, (total, tail), 1)
    terms = rows[:, width:].astype(jnp.float32)
    weight = jnp.sum(jnp.where(lane % (tail // 2) == slot, terms, 0.0), axis=1, keepdims=True)
    step = 256
    for at in range(0, units, step):
        gate = jnp.dot(rows[:, :width], gate_ref[:, at : at + step], preferred_element_type=jnp.float32)
        up = jnp.dot(rows[:, :width], up_ref[:, at : at + step], preferred_element_type=jnp.float32)
        value = gate / (1.0 + jnp.exp(-gate)) * up
        hidden[:, at : at + step] = (value * weight).astype(jnp.bfloat16)

    for at in range(0, width, 512):
        part = slice(at, at + 512)
        out = jnp.dot(hidden[...], down_ref[:, part], preferred_element_type=jnp.float32)
        out = out.astype(jnp.bfloat16)
        own_ref[:, part] = out[:count]
        near_ref[:, part] = out[count : 2 * count]
        for side in range(2):
            low, rows_of = (2 + side) * count, slice(side * count // 2, (side + 1) * count // 2)
            low_ref[rows_of, part] = out[low : low + count // 2]
            high_ref[rows_of, part] = out[low + count // 2 : low + count]


def run_expert(swapped, flags, weights, parts, plan):
    total = sum(high - low for _, low, high in plan)
    count = total // 4
    width, units = weights[0].shape
    weights = [pltpu.with_memory_space_constraint(w, pltpu.VMEM) for w in weights]
    return pl.pallas_call(
        functools.partial(expert_kernel, swapped, count, plan),
        out_shape=[jax.ShapeDtypeStruct((count, width), jnp.bfloat16)] * 4,
        in_specs=[pl.BlockSpec(memory_space=pltpu.SMEM)] + [in_vmem()] * (3 + len(parts)),
        out_specs=[in_vmem()] * 4,
        scratch_shapes=[
            pltpu.VMEM((total, parts[0].shape[1]), jnp.bfloat16),
            pltpu.VMEM((total, units), jnp.bfloat16),
        ],
        compiler_params=pltpu.CompilerParams(vmem_limit_bytes=16 * MIB),
        cost_estimate=pl.CostEstimate(
            flops=total * width * units * 6, bytes_accessed=4 * total * width, transcendentals=0
        ),
        name="expert",
    )(flags, *weights, *parts)


def add_kernel(first_ref, second_ref, sum_ref):
    sum_ref[...] = first_ref[...] + second_ref[...].astype(jnp.float32)


def add(first, second):
    return pl.pallas_call(
        add_kernel,
        out_shape=jax.ShapeDtypeStruct(first.shape, jnp.float32),
        in_specs=[in_vmem()] * 2,
        out_specs=in_vmem(),
        compiler_params=pltpu.CompilerParams(vmem_limit_bytes=4 * MIB),
        cost_estimate=pl.CostEstimate(flops=1 << 34, bytes_accessed=0, transcendentals=0),
        name="add",
    )(first, second)


def on_device(states, ids, probs, flags, w_gate, w_up, w_down):
    devices = lax.axis_size("expert")
    lines = devices // 4
    steps, tokens, width = states.shape

    def index(far, near, core):
        return far * 4 + near * 2 + core

    every = [(z, y, c) for z in range(lines) for y in range(2) for c in range(2)]

    def swap_core(x):
        return lax.ppermute(x, "expert", [(index(z, y, c), index(z, y, 1 - c)) for z, y, c in every])

    def swap_near(x):
        return lax.ppermute(x, "expert", [(index(z, y, c), index(z, 1 - y, c)) for z, y, c in every])

    def swap_far(x, by):
        return lax.ppermute(x, "expert", [(index(z, y, c), index(z ^ by, y, c)) for z, y, c in every])

    tail = 2 * devices
    tail = -(-tail // LANES) * LANES
    ids, probs = jnp.swapaxes(ids, 1, 2), jnp.swapaxes(probs, 1, 2)
    middle = lines // 2
    strides = [middle >> shift for shift in range(1, middle.bit_length())]
    head, half = middle * tokens, lines * tokens

    def grow(block, strides):
        for by in strides:
            block = jnp.concatenate([block, swap_far(block, by)])
        return block

    def places(strides):
        found = [0]
        for by in strides:
            found += [place ^ by for place in found]
        return found

    def collapse(block):
        for by in strides[::-1]:
            keep = block.shape[0] // 2
            block = block[:keep] + swap_far(block[keep:].astype(jnp.bfloat16), by).astype(jnp.float32)
        return block

    def after(x, *events):
        return lax.optimization_barrier((x, events))[0]

    w_gate, w_up, w_down = w_gate[0], w_up[0], w_down[0]
    messages = make_messages(states, ids, probs, tail)
    far = swap_far(messages[0], middle)
    others = [swap_far(messages[0], by) for by in places(strides)[1:]]
    near_own = [swap_near(message) for message in messages]
    loaded = load_weights(w_gate, w_up)
    loaded, near_own, others, far = lax.optimization_barrier((loaded, near_own, others, far))
    near_close = [swap_near(block) for block in others]
    crossed = [swap_far(after(message, far), middle) for message in messages[1:]]
    far = grow(far, strides)
    near_far = swap_near(far)
    last = load_weights(after(w_down, far))
    last, near_close, crossed = lax.optimization_barrier((last, near_close, crossed))
    loaded += last
    line = jnp.concatenate([messages[0], *others, far, near_own[0], *near_close])
    parts = [line, swap_core(line), near_far, swap_core(near_far)]
    near_crossed = [swap_near(block) for block in crossed]
    wanted = places(strides)
    wanted += [middle ^ place for place in wanted]
    found = places([middle] + strides)
    outputs, ready = [], far
    for step in range(steps):
        plan = []
        if step:
            rest = jnp.concatenate(arrived)
            line = jnp.concatenate([messages[step], crossed[step - 1], rest, near_own[step], near_crossed[step - 1], after(near_rest, ready)])
            parts = [line, swap_core(line)]
        for core in range(2):
            if step:
                for side in range(2):
                    at = [side * half + found.index(place) * tokens for place in wanted]
                    plan += [(core, row, row + tokens) for row in at]
            else:
                plan += [(core, 0, half + head), (2 + core, 0, head)]
        own, peer, other_low, other_high = run_expert(step > 0, flags, loaded, after(parts, ready), tuple(plan))
        if step:
            other_high = after(swap_core(other_high), near).astype(jnp.float32)
            other_low = swap_core(after(other_low, near))
        else:
            arrived, line = [], jnp.concatenate([messages[1], crossed[0]])
            for by in strides:
                arrived.append(after(swap_far(line, by), other_low))
                line = jnp.concatenate([line, arrived[-1]])
            near_rest = swap_near(jnp.concatenate(arrived))
            other_high, other_low = after((other_high, other_low), arrived)
            other_high = swap_core(other_high).astype(jnp.float32)
            other_low = swap_core(other_low)
        to_high = (peer[head:].astype(jnp.float32) + other_high[head:]).astype(jnp.bfloat16)
        other_low = after(other_low, to_high).astype(jnp.float32)
        to_low = (peer[:head].astype(jnp.float32) + other_low[head:]).astype(jnp.bfloat16)
        ready = to_high, to_low
        if step:
            near = after(near, other_low).astype(jnp.float32)
            high += near[head:]
            low += near[:head]
            for by in strides[::-1]:
                keep = high.shape[0] // 2
                sent = jnp.concatenate([low[keep:], high[keep:]]).astype(jnp.bfloat16)
                sent = swap_far(sent, by).astype(jnp.float32)
                low, high = low[:keep] + sent[:keep], high[:keep] + sent[keep:]
            outputs.append((low, swap_far(high.astype(jnp.bfloat16), middle)))
        high = own[head:].astype(jnp.float32) + other_high[:head]
        low = own[:head].astype(jnp.float32) + other_low[:head]
        if step + 1 < steps:
            near = swap_near(jnp.concatenate([to_low, to_high]))
    near_high = swap_near(to_high)
    near = swap_near(after(to_low, near_high))
    outputs = [low + after(high, near).astype(jnp.float32) for low, high in outputs]
    high = collapse(high + near_high.astype(jnp.float32))
    low += after(near, high).astype(jnp.float32)
    first = add(low[:tokens], swap_far(high.astype(jnp.bfloat16), middle))
    outputs.append(collapse(jnp.concatenate([first, low[tokens:]])))
    return jnp.stack(outputs).astype(jnp.bfloat16)


def solution(mesh):
    rows = P(None, ("groups", "expert"), None)
    weights = P("expert", None, None)
    return jax.shard_map(
        on_device,
        mesh=mesh,
        in_specs=(rows, rows, rows, P(), weights, weights, weights),
        out_specs=rows,
        check_vma=False,
    )
```

```python
import functools

import jax
import jax.numpy as jnp
from jax import lax
from jax.experimental import pallas as pl
from jax.experimental.pallas import tpu as pltpu
from jax.sharding import PartitionSpec as P

LANES = 128
MIB = 1 << 20


def in_vmem():
    return pl.BlockSpec(memory_space=pltpu.VMEM)


def message_kernel(states_ref, ids_ref, probs_ref, *message_refs):
    steps, tokens, width = states_ref.shape
    tail = message_refs[0].shape[1] - width
    half = tail // 2
    place = lax.broadcasted_iota(jnp.int32, (tail, tokens), 0)
    row = lax.broadcasted_iota(jnp.int32, (tokens, tokens), 0)
    column = lax.broadcasted_iota(jnp.int32, (tokens, tokens), 1)
    one = jnp.where(row == column, 1.0, 0.0).astype(jnp.bfloat16)
    for step in range(steps):
        probs = probs_ref[step]
        share = probs / jnp.sum(probs, axis=0, keepdims=True)
        ids = ids_ref[step]
        dense = jnp.zeros((tail, tokens), jnp.float32)
        for k in range(ids.shape[0]):
            dense += jnp.where(ids[k : k + 1] == place % half, share[k : k + 1], 0.0)
        high = dense.astype(jnp.bfloat16).astype(jnp.float32)
        terms = jnp.where(place < half, high, dense - high).astype(jnp.bfloat16)
        upright = lax.dot_general(one, terms, (((1,), (1,)), ((), ())), preferred_element_type=jnp.float32)
        upright = upright.astype(jnp.bfloat16)
        message_refs[step][:, :width] = states_ref[step]
        message_refs[step][:, width:] = upright


def make_messages(states, ids, probs, tail):
    steps, tokens, width = states.shape
    states, ids, probs = (pltpu.with_memory_space_constraint(x, pltpu.HBM) for x in (states, ids, probs))

    def whole(shape):
        return pl.BlockSpec(shape, lambda i: (0,) * len(shape))

    shapes = [(tokens, width + tail)] * steps
    return pl.pallas_call(
        message_kernel,
        grid=(1,),
        out_shape=[jax.ShapeDtypeStruct(shape, jnp.bfloat16) for shape in shapes],
        in_specs=[whole(x.shape) for x in (states, ids, probs)],
        out_specs=[whole(shape) for shape in shapes],
        compiler_params=pltpu.CompilerParams(vmem_limit_bytes=4 * MIB),
        name="messages",
    )(states, ids, probs)


def load_kernel(*refs):
    count = len(refs) // 3
    copies = [
        pltpu.make_async_copy(refs[i], refs[count + i], refs[2 * count + i]) for i in range(count)
    ]
    for copy in copies:
        copy.start()
    for copy in copies:
        copy.wait()


def load_weights(*arrays):
    arrays = [pltpu.with_memory_space_constraint(x, pltpu.HBM) for x in arrays]
    return pl.pallas_call(
        load_kernel,
        out_shape=[pltpu.VMEM(x.shape, x.dtype) for x in arrays],
        in_specs=[pl.BlockSpec(memory_space=pltpu.HBM)] * len(arrays),
        out_specs=[in_vmem()] * len(arrays),
        scratch_shapes=[pltpu.SemaphoreType.DMA(())] * len(arrays),
        cost_estimate=pl.CostEstimate(flops=0, bytes_accessed=0, transcendentals=0),
        compiler_params=pltpu.CompilerParams(vmem_limit_bytes=4 * MIB),
        name="load_weights",
    )(*arrays)


def expert_kernel(swapped, count, plan, flags_ref, gate_ref, up_ref, down_ref, *refs):
    *sources, own_ref, near_ref, low_ref, high_ref, rows, hidden = refs
    width, units = gate_ref.shape
    tail = rows.shape[1] - width
    owner = lax.axis_index("expert")
    slot = jnp.bitwise_xor(owner, flags_ref[owner]) if swapped else owner
    at = 0
    for source, low, high in plan:
        rows[at : at + high - low] = sources[source][low:high]
        at += high - low
    total = rows.shape[0]
    lane = lax.broadcasted_iota(jnp.int32, (total, tail), 1)
    terms = rows[:, width:].astype(jnp.float32)
    weight = jnp.sum(jnp.where(lane % (tail // 2) == slot, terms, 0.0), axis=1, keepdims=True)
    step = 256
    for at in range(0, units, step):
        gate = jnp.dot(rows[:, :width], gate_ref[:, at : at + step], preferred_element_type=jnp.float32)
        up = jnp.dot(rows[:, :width], up_ref[:, at : at + step], preferred_element_type=jnp.float32)
        value = gate / (1.0 + jnp.exp(-gate)) * up
        hidden[:, at : at + step] = (value * weight).astype(jnp.bfloat16)

    for at in range(0, width, 512):
        part = slice(at, at + 512)
        out = jnp.dot(hidden[...], down_ref[:, part], preferred_element_type=jnp.float32)
        out = out.astype(jnp.bfloat16)
        own_ref[:, part] = out[:count]
        near_ref[:, part] = out[count : 2 * count]
        for side in range(2):
            low, rows_of = (2 + side) * count, slice(side * count // 2, (side + 1) * count // 2)
            low_ref[rows_of, part] = out[low : low + count // 2]
            high_ref[rows_of, part] = out[low + count // 2 : low + count]


def run_expert(swapped, flags, weights, parts, plan):
    total = sum(high - low for _, low, high in plan)
    count = total // 4
    width, units = weights[0].shape
    weights = [pltpu.with_memory_space_constraint(w, pltpu.VMEM) for w in weights]
    return pl.pallas_call(
        functools.partial(expert_kernel, swapped, count, plan),
        out_shape=[jax.ShapeDtypeStruct((count, width), jnp.bfloat16)] * 4,
        in_specs=[pl.BlockSpec(memory_space=pltpu.SMEM)] + [in_vmem()] * (3 + len(parts)),
        out_specs=[in_vmem()] * 4,
        scratch_shapes=[
            pltpu.VMEM((total, parts[0].shape[1]), jnp.bfloat16),
            pltpu.VMEM((total, units), jnp.bfloat16),
        ],
        compiler_params=pltpu.CompilerParams(vmem_limit_bytes=16 * MIB),
        cost_estimate=pl.CostEstimate(
            flops=total * width * units * 6, bytes_accessed=4 * total * width, transcendentals=0
        ),
        name="expert",
    )(flags, *weights, *parts)


def add_kernel(first_ref, second_ref, sum_ref):
    sum_ref[...] = first_ref[...] + second_ref[...].astype(jnp.float32)


def add(first, second):
    return pl.pallas_call(
        add_kernel,
        out_shape=jax.ShapeDtypeStruct(first.shape, jnp.float32),
        in_specs=[in_vmem()] * 2,
        out_specs=in_vmem(),
        compiler_params=pltpu.CompilerParams(vmem_limit_bytes=4 * MIB),
        cost_estimate=pl.CostEstimate(flops=1 << 34, bytes_accessed=0, transcendentals=0),
        name="add",
    )(first, second)


def on_device(states, ids, probs, flags, w_gate, w_up, w_down):
    devices = lax.axis_size("expert")
    lines = devices // 4
    steps, tokens, width = states.shape

    def index(far, near, core):
        return far * 4 + near * 2 + core

    every = [(z, y, c) for z in range(lines) for y in range(2) for c in range(2)]

    def swap_core(x):
        return lax.ppermute(x, "expert", [(index(z, y, c), index(z, y, 1 - c)) for z, y, c in every])

    def swap_near(x):
        return lax.ppermute(x, "expert", [(index(z, y, c), index(z, 1 - y, c)) for z, y, c in every])

    def swap_far(x, by):
        return lax.ppermute(x, "expert", [(index(z, y, c), index(z ^ by, y, c)) for z, y, c in every])

    tail = 2 * devices
    tail = -(-tail // LANES) * LANES
    ids, probs = jnp.swapaxes(ids, 1, 2), jnp.swapaxes(probs, 1, 2)
    middle = lines // 2
    strides = [middle >> shift for shift in range(1, middle.bit_length())]
    head, half = middle * tokens, lines * tokens

    def grow(block, strides):
        for by in strides:
            block = jnp.concatenate([block, swap_far(block, by)])
        return block

    def places(strides):
        found = [0]
        for by in strides:
            found += [place ^ by for place in found]
        return found

    def collapse(block):
        for by in strides[::-1]:
            keep = block.shape[0] // 2
            block = block[:keep] + swap_far(block[keep:].astype(jnp.bfloat16), by).astype(jnp.float32)
        return block

    def after(x, *events):
        return lax.optimization_barrier((x, events))[0]

    w_gate, w_up, w_down = w_gate[0], w_up[0], w_down[0]
    messages = make_messages(states, ids, probs, tail)
    far = swap_far(messages[0], middle)
    others = [swap_far(messages[0], by) for by in places(strides)[1:]]
    near_own = [swap_near(message) for message in messages]
    loaded = load_weights(w_gate, w_up)
    later = [[swap_far(message, by) for by in places(strides)[1:]] for message in messages[1:]]
    near_own, later, loaded, others, far = lax.optimization_barrier((near_own, later, loaded, others, far))
    near_close = [swap_near(block) for block in others]
    crossed = [swap_far(after(message, far), middle) for message in messages[1:]]
    far = grow(far, strides)
    near_far = swap_near(far)
    last = load_weights(after(w_down, far))
    last, near_close, crossed = lax.optimization_barrier((last, near_close, crossed))
    loaded += last
    line = jnp.concatenate([messages[0], *others, far, near_own[0], *near_close])
    parts = [line, swap_core(line), near_far, swap_core(near_far)]
    next_line, next_near = [], []
    for step in range(1, steps):
        block, rest = crossed[step - 1], []
        near_block = swap_near(block)
        for by in strides:
            rest.append(after(swap_far(block, by), near_far))
            block = jnp.concatenate([block, rest[-1]])
        near_rest = swap_near(jnp.concatenate([*later[step - 1], *rest]))
        next_line.append([messages[step], *later[step - 1], block])
        next_near.append([near_own[step], near_block, near_rest])
    outputs, ready = [], far
    for step in range(steps):
        plan = []
        if step:
            near_first, near_block, near_rest = next_near[step - 1]
            near_rest = after(near_rest, ready)
            cut = head - tokens
            line = [*next_line[step - 1], near_first, near_rest[:cut], near_block, near_rest[cut:]]
            line = jnp.concatenate(line)
            parts = [line, swap_core(line)]
        for core in range(2):
            plan += [(core, 0, 2 * half)] if step else [(core, 0, half + head), (2 + core, 0, head)]
        own, peer, other_low, other_high = run_expert(step > 0, flags, loaded, after(parts, ready), tuple(plan))
        if step:
            other_high = after(swap_core(other_high), near).astype(jnp.float32)
            other_low = swap_core(after(other_low, near))
        else:
            other_high, other_low = after((other_high, other_low), next_near[0][2])
            other_high = swap_core(other_high).astype(jnp.float32)
            other_low = swap_core(other_low)
        to_high = (peer[head:].astype(jnp.float32) + other_high[head:]).astype(jnp.bfloat16)
        other_low = after(other_low, to_high).astype(jnp.float32)
        to_low = (peer[:head].astype(jnp.float32) + other_low[head:]).astype(jnp.bfloat16)
        ready = to_high, to_low
        if step:
            near = after(near, other_low).astype(jnp.float32)
            high += near[head:]
            low += near[:head]
            for by in strides[::-1]:
                keep = high.shape[0] // 2
                sent = jnp.concatenate([low[keep:], high[keep:]]).astype(jnp.bfloat16)
                sent = swap_far(sent, by).astype(jnp.float32)
                low, high = low[:keep] + sent[:keep], high[:keep] + sent[keep:]
            outputs.append((low, swap_far(high.astype(jnp.bfloat16), middle)))
        high = own[head:].astype(jnp.float32) + other_high[:head]
        low = own[:head].astype(jnp.float32) + other_low[:head]
        if step + 1 < steps:
            near = swap_near(jnp.concatenate([to_low, to_high]))
    near_high = swap_near(to_high)
    near = swap_near(after(to_low, near_high))
    outputs = [low + after(high, near).astype(jnp.float32) for low, high in outputs]
    high = collapse(high + near_high.astype(jnp.float32))
    low += after(near, high).astype(jnp.float32)
    first = add(low[:tokens], swap_far(high.astype(jnp.bfloat16), middle))
    outputs.append(collapse(jnp.concatenate([first, low[tokens:]])))
    return jnp.stack(outputs).astype(jnp.bfloat16)


def solution(mesh):
    rows = P(None, ("groups", "expert"), None)
    weights = P("expert", None, None)
    return jax.shard_map(
        on_device,
        mesh=mesh,
        in_specs=(rows, rows, rows, P(), weights, weights, weights),
        out_specs=rows,
        check_vma=False,
    )
```

```python
import functools

import jax
import jax.numpy as jnp
from jax import lax
from jax.experimental import pallas as pl
from jax.experimental.pallas import tpu as pltpu
from jax.sharding import PartitionSpec as P

LANES = 128
MIB = 1 << 20


def in_vmem():
    return pl.BlockSpec(memory_space=pltpu.VMEM)


def message_kernel(states_ref, ids_ref, probs_ref, *message_refs):
    steps, tokens, width = states_ref.shape
    tail = message_refs[0].shape[1] - width
    half = tail // 2
    place = lax.broadcasted_iota(jnp.int32, (tail, tokens), 0)
    row = lax.broadcasted_iota(jnp.int32, (tokens, tokens), 0)
    column = lax.broadcasted_iota(jnp.int32, (tokens, tokens), 1)
    one = jnp.where(row == column, 1.0, 0.0).astype(jnp.bfloat16)
    for step in range(steps):
        probs = probs_ref[step]
        share = probs / jnp.sum(probs, axis=0, keepdims=True)
        ids = ids_ref[step]
        dense = jnp.zeros((tail, tokens), jnp.float32)
        for k in range(ids.shape[0]):
            dense += jnp.where(ids[k : k + 1] == place % half, share[k : k + 1], 0.0)
        high = dense.astype(jnp.bfloat16).astype(jnp.float32)
        terms = jnp.where(place < half, high, dense - high).astype(jnp.bfloat16)
        upright = lax.dot_general(one, terms, (((1,), (1,)), ((), ())), preferred_element_type=jnp.float32)
        upright = upright.astype(jnp.bfloat16)
        message_refs[step][:, :width] = states_ref[step]
        message_refs[step][:, width:] = upright


def make_messages(states, ids, probs, tail):
    steps, tokens, width = states.shape
    states, ids, probs = (pltpu.with_memory_space_constraint(x, pltpu.HBM) for x in (states, ids, probs))

    def whole(shape):
        return pl.BlockSpec(shape, lambda i: (0,) * len(shape))

    shapes = [(tokens, width + tail)] * steps
    return pl.pallas_call(
        message_kernel,
        grid=(1,),
        out_shape=[jax.ShapeDtypeStruct(shape, jnp.bfloat16) for shape in shapes],
        in_specs=[whole(x.shape) for x in (states, ids, probs)],
        out_specs=[whole(shape) for shape in shapes],
        compiler_params=pltpu.CompilerParams(vmem_limit_bytes=4 * MIB),
        name="messages",
    )(states, ids, probs)


def load_kernel(*refs):
    count = len(refs) // 3
    copies = [
        pltpu.make_async_copy(refs[i], refs[count + i], refs[2 * count + i]) for i in range(count)
    ]
    for copy in copies:
        copy.start()
    for copy in copies:
        copy.wait()


def load_weights(*arrays):
    arrays = [pltpu.with_memory_space_constraint(x, pltpu.HBM) for x in arrays]
    return pl.pallas_call(
        load_kernel,
        out_shape=[pltpu.VMEM(x.shape, x.dtype) for x in arrays],
        in_specs=[pl.BlockSpec(memory_space=pltpu.HBM)] * len(arrays),
        out_specs=[in_vmem()] * len(arrays),
        scratch_shapes=[pltpu.SemaphoreType.DMA(())] * len(arrays),
        cost_estimate=pl.CostEstimate(flops=0, bytes_accessed=0, transcendentals=0),
        compiler_params=pltpu.CompilerParams(vmem_limit_bytes=4 * MIB),
        name="load_weights",
    )(*arrays)


def expert_kernel(swapped, count, plan, flags_ref, gate_ref, up_ref, down_ref, *refs):
    *sources, own_ref, near_ref, low_ref, high_ref, rows, hidden = refs
    width, units = gate_ref.shape
    tail = rows.shape[1] - width
    owner = lax.axis_index("expert")
    slot = jnp.bitwise_xor(owner, flags_ref[owner]) if swapped else owner
    at = 0
    for source, low, high in plan:
        rows[at : at + high - low] = sources[source][low:high]
        at += high - low
    total = rows.shape[0]
    lane = lax.broadcasted_iota(jnp.int32, (total, tail), 1)
    terms = rows[:, width:].astype(jnp.float32)
    weight = jnp.sum(jnp.where(lane % (tail // 2) == slot, terms, 0.0), axis=1, keepdims=True)
    step = 256
    for at in range(0, units, step):
        gate = jnp.dot(rows[:, :width], gate_ref[:, at : at + step], preferred_element_type=jnp.float32)
        up = jnp.dot(rows[:, :width], up_ref[:, at : at + step], preferred_element_type=jnp.float32)
        value = gate / (1.0 + jnp.exp(-gate)) * up
        hidden[:, at : at + step] = (value * weight).astype(jnp.bfloat16)

    for at in range(0, width, 512):
        part = slice(at, at + 512)
        out = jnp.dot(hidden[...], down_ref[:, part], preferred_element_type=jnp.float32)
        out = out.astype(jnp.bfloat16)
        own_ref[:, part] = out[:count]
        near_ref[:, part] = out[count : 2 * count]
        for side in range(2):
            low, rows_of = (2 + side) * count, slice(side * count // 2, (side + 1) * count // 2)
            low_ref[rows_of, part] = out[low : low + count // 2]
            high_ref[rows_of, part] = out[low + count // 2 : low + count]


def run_expert(swapped, flags, weights, parts, plan):
    total = sum(high - low for _, low, high in plan)
    count = total // 4
    width, units = weights[0].shape
    weights = [pltpu.with_memory_space_constraint(w, pltpu.VMEM) for w in weights]
    return pl.pallas_call(
        functools.partial(expert_kernel, swapped, count, plan),
        out_shape=[jax.ShapeDtypeStruct((count, width), jnp.bfloat16)] * 4,
        in_specs=[pl.BlockSpec(memory_space=pltpu.SMEM)] + [in_vmem()] * (3 + len(parts)),
        out_specs=[in_vmem()] * 4,
        scratch_shapes=[
            pltpu.VMEM((total, parts[0].shape[1]), jnp.bfloat16),
            pltpu.VMEM((total, units), jnp.bfloat16),
        ],
        compiler_params=pltpu.CompilerParams(vmem_limit_bytes=16 * MIB),
        cost_estimate=pl.CostEstimate(
            flops=total * width * units * 6, bytes_accessed=4 * total * width, transcendentals=0
        ),
        name="expert",
    )(flags, *weights, *parts)


def add_kernel(first_ref, second_ref, sum_ref):
    sum_ref[...] = first_ref[...] + second_ref[...].astype(jnp.float32)


def add(first, second):
    return pl.pallas_call(
        add_kernel,
        out_shape=jax.ShapeDtypeStruct(first.shape, jnp.float32),
        in_specs=[in_vmem()] * 2,
        out_specs=in_vmem(),
        compiler_params=pltpu.CompilerParams(vmem_limit_bytes=4 * MIB),
        cost_estimate=pl.CostEstimate(flops=1 << 34, bytes_accessed=0, transcendentals=0),
        name="add",
    )(first, second)


def on_device(states, ids, probs, flags, w_gate, w_up, w_down):
    devices = lax.axis_size("expert")
    lines = devices // 4
    steps, tokens, width = states.shape

    def index(far, near, core):
        return far * 4 + near * 2 + core

    every = [(z, y, c) for z in range(lines) for y in range(2) for c in range(2)]

    def swap_core(x):
        return lax.ppermute(x, "expert", [(index(z, y, c), index(z, y, 1 - c)) for z, y, c in every])

    def swap_near(x):
        return lax.ppermute(x, "expert", [(index(z, y, c), index(z, 1 - y, c)) for z, y, c in every])

    def swap_far(x, by):
        return lax.ppermute(x, "expert", [(index(z, y, c), index(z ^ by, y, c)) for z, y, c in every])

    tail = 2 * devices
    tail = -(-tail // LANES) * LANES
    ids, probs = jnp.swapaxes(ids, 1, 2), jnp.swapaxes(probs, 1, 2)
    middle = lines // 2
    strides = [middle >> shift for shift in range(1, middle.bit_length())]
    head, half = middle * tokens, lines * tokens

    def grow(block, strides):
        for by in strides:
            block = jnp.concatenate([block, swap_far(block, by)])
        return block

    def places(strides):
        found = [0]
        for by in strides:
            found += [place ^ by for place in found]
        return found

    def collapse(block):
        for by in strides[::-1]:
            keep = block.shape[0] // 2
            block = block[:keep] + swap_far(block[keep:].astype(jnp.bfloat16), by).astype(jnp.float32)
        return block

    def after(x, *events):
        return lax.optimization_barrier((x, events))[0]

    w_gate, w_up, w_down = w_gate[0], w_up[0], w_down[0]
    messages = make_messages(states, ids, probs, tail)
    far = swap_far(messages[0], middle)
    others = [swap_far(messages[0], by) for by in places(strides)[1:]]
    near_own = [swap_near(message) for message in messages]
    loaded = load_weights(w_gate, w_up)
    later = [[swap_far(message, by) for by in places(strides)[1:]] for message in messages[1:]]
    near_own, later, loaded, others, far = lax.optimization_barrier((near_own, later, loaded, others, far))
    near_close = swap_near(jnp.concatenate(sum(later, others)))
    crossed = [swap_far(after(message, far), middle) for message in messages[1:]]
    far = grow(far, strides)
    near_far = swap_near(far)
    last = load_weights(after(w_down, far))
    last, near_close, crossed = lax.optimization_barrier((last, near_close, crossed))
    loaded += last
    cut = head - tokens
    line = jnp.concatenate([messages[0], *others, far, near_own[0], near_close[:cut]])
    parts = [line, swap_core(line), near_far, swap_core(near_far)]
    next_line, next_near = [], []
    for step in range(1, steps):
        block, rest = crossed[step - 1], []
        near_block = swap_near(block)
        for by in strides:
            rest.append(after(swap_far(block, by), near_far))
            block = jnp.concatenate([block, rest[-1]])
        near_rest = swap_near(jnp.concatenate(rest))
        next_line.append([messages[step], *later[step - 1], block, near_own[step]])
        next_line[-1] += [near_close[step * cut : (step + 1) * cut], near_block]
        next_near.append(near_rest)
    outputs, ready = [], far
    for step in range(steps):
        plan = []
        if step:
            line = jnp.concatenate([*next_line[step - 1], after(next_near[step - 1], ready)])
            parts = [line, swap_core(line)]
        for core in range(2):
            plan += [(core, 0, 2 * half)] if step else [(core, 0, half + head), (2 + core, 0, head)]
        own, peer, other_low, other_high = run_expert(step > 0, flags, loaded, after(parts, ready), tuple(plan))
        if step:
            other_high = after(swap_core(other_high), near).astype(jnp.float32)
            other_low = swap_core(after(other_low, near))
        else:
            other_high, other_low = after((other_high, other_low), next_near[0])
            other_high = swap_core(other_high).astype(jnp.float32)
            other_low = swap_core(other_low)
        to_high = (peer[head:].astype(jnp.float32) + other_high[head:]).astype(jnp.bfloat16)
        other_low = after(other_low, to_high).astype(jnp.float32)
        to_low = (peer[:head].astype(jnp.float32) + other_low[head:]).astype(jnp.bfloat16)
        ready = to_high, to_low
        if step:
            near = after(near, other_low).astype(jnp.float32)
            hop = collapse(high + near[head:])
            low += after(near[:head], hop)
            outputs.append((collapse(low), swap_far(hop.astype(jnp.bfloat16), middle)))
        high = own[head:].astype(jnp.float32) + other_high[:head]
        low = own[:head].astype(jnp.float32) + other_low[:head]
        if step + 1 < steps:
            near = swap_near(jnp.concatenate([to_low, to_high]))
    near_high = swap_near(to_high)
    near = swap_near(after(to_low, near_high))
    outputs = [low + after(high, near).astype(jnp.float32) for low, high in outputs]
    high = collapse(high + after(near_high, hop).astype(jnp.float32))
    low += after(near, high).astype(jnp.float32)
    first = add(low[:tokens], swap_far(high.astype(jnp.bfloat16), middle))
    outputs.append(collapse(jnp.concatenate([first, low[tokens:]])))
    return jnp.stack(outputs).astype(jnp.bfloat16)


def solution(mesh):
    rows = P(None, ("groups", "expert"), None)
    weights = P("expert", None, None)
    return jax.shard_map(
        on_device,
        mesh=mesh,
        in_specs=(rows, rows, rows, P(), weights, weights, weights),
        out_specs=rows,
        check_vma=False,
    )
```

```python
import functools

import jax
import jax.numpy as jnp
from jax import lax
from jax.experimental import pallas as pl
from jax.experimental.pallas import tpu as pltpu
from jax.sharding import PartitionSpec as P

LANES = 128
MIB = 1 << 20


def in_vmem():
    return pl.BlockSpec(memory_space=pltpu.VMEM)


def message_kernel(states_ref, ids_ref, probs_ref, *message_refs):
    steps, tokens, width = states_ref.shape
    tail = message_refs[0].shape[1] - width
    half = tail // 2
    place = lax.broadcasted_iota(jnp.int32, (tail, tokens), 0)
    row = lax.broadcasted_iota(jnp.int32, (tokens, tokens), 0)
    column = lax.broadcasted_iota(jnp.int32, (tokens, tokens), 1)
    one = jnp.where(row == column, 1.0, 0.0).astype(jnp.bfloat16)
    for step in range(steps):
        probs = probs_ref[step]
        share = probs / jnp.sum(probs, axis=0, keepdims=True)
        ids = ids_ref[step]
        dense = jnp.zeros((tail, tokens), jnp.float32)
        for k in range(ids.shape[0]):
            dense += jnp.where(ids[k : k + 1] == place % half, share[k : k + 1], 0.0)
        high = dense.astype(jnp.bfloat16).astype(jnp.float32)
        terms = jnp.where(place < half, high, dense - high).astype(jnp.bfloat16)
        upright = lax.dot_general(one, terms, (((1,), (1,)), ((), ())), preferred_element_type=jnp.float32)
        upright = upright.astype(jnp.bfloat16)
        message_refs[step][:, :width] = states_ref[step]
        message_refs[step][:, width:] = upright


def make_messages(states, ids, probs, tail):
    steps, tokens, width = states.shape
    states, ids, probs = (pltpu.with_memory_space_constraint(x, pltpu.HBM) for x in (states, ids, probs))

    def whole(shape):
        return pl.BlockSpec(shape, lambda i: (0,) * len(shape))

    shapes = [(tokens, width + tail)] * steps
    return pl.pallas_call(
        message_kernel,
        grid=(1,),
        out_shape=[jax.ShapeDtypeStruct(shape, jnp.bfloat16) for shape in shapes],
        in_specs=[whole(x.shape) for x in (states, ids, probs)],
        out_specs=[whole(shape) for shape in shapes],
        compiler_params=pltpu.CompilerParams(vmem_limit_bytes=4 * MIB),
        name="messages",
    )(states, ids, probs)


def load_kernel(*refs):
    count = len(refs) // 3
    copies = [
        pltpu.make_async_copy(refs[i], refs[count + i], refs[2 * count + i]) for i in range(count)
    ]
    for copy in copies:
        copy.start()
    for copy in copies:
        copy.wait()


def load_weights(*arrays):
    arrays = [pltpu.with_memory_space_constraint(x, pltpu.HBM) for x in arrays]
    return pl.pallas_call(
        load_kernel,
        out_shape=[pltpu.VMEM(x.shape, x.dtype) for x in arrays],
        in_specs=[pl.BlockSpec(memory_space=pltpu.HBM)] * len(arrays),
        out_specs=[in_vmem()] * len(arrays),
        scratch_shapes=[pltpu.SemaphoreType.DMA(())] * len(arrays),
        cost_estimate=pl.CostEstimate(flops=0, bytes_accessed=0, transcendentals=0),
        compiler_params=pltpu.CompilerParams(vmem_limit_bytes=4 * MIB),
        name="load_weights",
    )(*arrays)


def expert_kernel(swapped, count, plan, flags_ref, gate_ref, up_ref, down_ref, *refs):
    *sources, own_ref, near_ref, low_ref, high_ref, rows, hidden = refs
    width, units = gate_ref.shape
    tail = rows.shape[1] - width
    owner = lax.axis_index("expert")
    slot = jnp.bitwise_xor(owner, flags_ref[owner]) if swapped else owner
    at = 0
    for source, low, high in plan:
        rows[at : at + high - low] = sources[source][low:high]
        at += high - low
    total = rows.shape[0]
    lane = lax.broadcasted_iota(jnp.int32, (total, tail), 1)
    terms = rows[:, width:].astype(jnp.float32)
    weight = jnp.sum(jnp.where(lane % (tail // 2) == slot, terms, 0.0), axis=1, keepdims=True)
    step = 256
    for at in range(0, units, step):
        gate = jnp.dot(rows[:, :width], gate_ref[:, at : at + step], preferred_element_type=jnp.float32)
        up = jnp.dot(rows[:, :width], up_ref[:, at : at + step], preferred_element_type=jnp.float32)
        value = gate / (1.0 + jnp.exp(-gate)) * up
        hidden[:, at : at + step] = (value * weight).astype(jnp.bfloat16)

    for at in range(0, width, 512):
        part = slice(at, at + 512)
        out = jnp.dot(hidden[...], down_ref[:, part], preferred_element_type=jnp.float32)
        out = out.astype(jnp.bfloat16)
        own_ref[:, part] = out[:count]
        near_ref[:, part] = out[count : 2 * count]
        for side in range(2):
            low, rows_of = (2 + side) * count, slice(side * count // 2, (side + 1) * count // 2)
            low_ref[rows_of, part] = out[low : low + count // 2]
            high_ref[rows_of, part] = out[low + count // 2 : low + count]


def run_expert(swapped, flags, weights, parts, plan):
    total = sum(high - low for _, low, high in plan)
    count = total // 4
    width, units = weights[0].shape
    weights = [pltpu.with_memory_space_constraint(w, pltpu.VMEM) for w in weights]
    return pl.pallas_call(
        functools.partial(expert_kernel, swapped, count, plan),
        out_shape=[jax.ShapeDtypeStruct((count, width), jnp.bfloat16)] * 4,
        in_specs=[pl.BlockSpec(memory_space=pltpu.SMEM)] + [in_vmem()] * (3 + len(parts)),
        out_specs=[in_vmem()] * 4,
        scratch_shapes=[
            pltpu.VMEM((total, parts[0].shape[1]), jnp.bfloat16),
            pltpu.VMEM((total, units), jnp.bfloat16),
        ],
        compiler_params=pltpu.CompilerParams(vmem_limit_bytes=16 * MIB),
        cost_estimate=pl.CostEstimate(
            flops=total * width * units * 6, bytes_accessed=4 * total * width, transcendentals=0
        ),
        name="expert",
    )(flags, *weights, *parts)


def add_kernel(first_ref, second_ref, sum_ref):
    sum_ref[...] = first_ref[...] + second_ref[...].astype(jnp.float32)


def add(first, second):
    return pl.pallas_call(
        add_kernel,
        out_shape=jax.ShapeDtypeStruct(first.shape, jnp.float32),
        in_specs=[in_vmem()] * 2,
        out_specs=in_vmem(),
        compiler_params=pltpu.CompilerParams(vmem_limit_bytes=4 * MIB),
        cost_estimate=pl.CostEstimate(flops=1 << 34, bytes_accessed=0, transcendentals=0),
        name="add",
    )(first, second)


def on_device(states, ids, probs, flags, w_gate, w_up, w_down):
    devices = lax.axis_size("expert")
    lines = devices // 4
    steps, tokens, width = states.shape

    def index(far, near, core):
        return far * 4 + near * 2 + core

    every = [(z, y, c) for z in range(lines) for y in range(2) for c in range(2)]

    def swap_core(x):
        return lax.ppermute(x, "expert", [(index(z, y, c), index(z, y, 1 - c)) for z, y, c in every])

    def swap_near(x):
        return lax.ppermute(x, "expert", [(index(z, y, c), index(z, 1 - y, c)) for z, y, c in every])

    def swap_far(x, by):
        return lax.ppermute(x, "expert", [(index(z, y, c), index(z ^ by, y, c)) for z, y, c in every])

    tail = 2 * devices
    tail = -(-tail // LANES) * LANES
    ids, probs = jnp.swapaxes(ids, 1, 2), jnp.swapaxes(probs, 1, 2)
    middle = lines // 2
    strides = [middle >> shift for shift in range(1, middle.bit_length())]
    head, half = middle * tokens, lines * tokens

    def grow(block, strides):
        for by in strides:
            block = jnp.concatenate([block, swap_far(block, by)])
        return block

    def places(strides):
        found = [0]
        for by in strides:
            found += [place ^ by for place in found]
        return found

    def collapse(block):
        for by in strides[::-1]:
            keep = block.shape[0] // 2
            block = block[:keep] + swap_far(block[keep:].astype(jnp.bfloat16), by).astype(jnp.float32)
        return block

    def after(x, *events):
        return lax.optimization_barrier((x, events))[0]

    w_gate, w_up, w_down = w_gate[0], w_up[0], w_down[0]
    messages = make_messages(states, ids, probs, tail)
    far = swap_far(messages[0], middle)
    close = [messages[0], *[swap_far(messages[0], by) for by in places(strides)[1:]]]
    near_close = [swap_near(messages[0])]
    loaded = load_weights(w_gate, w_up)
    far, close, near_close, loaded = lax.optimization_barrier((far, close, near_close, loaded))
    others = close[1:]
    near_close += [swap_near(block) for block in others]
    crossed = [swap_far(after(message, far), middle) for message in messages[1:]]
    far = grow(far, strides)
    near_far = swap_near(far)
    last = load_weights(after(w_down, far))
    near_own = [swap_near(after(message, others)) for message in messages[1:]]
    crossed, near_close, near_own, last = lax.optimization_barrier((crossed, near_close, near_own, last))
    loaded += last
    line = jnp.concatenate([*close, far, *near_close])
    sources = [[line, swap_core(line), near_far, swap_core(near_far)]]
    wanted = places(strides)
    wanted += [middle ^ place for place in wanted]
    found = places([middle] + strides)
    for message, block, near in zip(messages[1:], crossed, near_own):
        line = grow(jnp.concatenate([message, block]), strides)
        near_line = swap_near(line[tokens:])
        line = jnp.concatenate([line, near])
        sources.append([line, near_line])
    outputs, ready = [], [source[0] for source in sources]
    for step in range(steps):
        plan = []
        for core in range(2):
            if step:
                at = [found.index(place) * tokens for place in wanted]
                plan += [(core, low, low + tokens) for low in at] + [(core, half, half + tokens)]
                plan += [(2 + core, low - tokens, low) for low in at[1:]]
            else:
                plan += [(core, 0, half + head), (2 + core, 0, head)]
        parts = sources[step]
        if step:
            line, near_line = after(sources[step], ready)
            parts = [line, swap_core(line), near_line, swap_core(near_line)]
        own, peer, other_low, other_high = run_expert(step > 0, flags, loaded, after(parts, ready), tuple(plan))
        other_high = swap_core(other_high if step else after(other_high, sources[1][1]))
        if step:
            other_high = after(other_high, near)
        other_high = other_high.astype(jnp.float32)
        other_low = swap_core(after(other_low, near if step else sources[1][1]))
        to_high = (peer[head:].astype(jnp.float32) + other_high[head:]).astype(jnp.bfloat16)
        other_low = after(other_low, to_high).astype(jnp.float32)
        to_low = (peer[:head].astype(jnp.float32) + other_low[head:]).astype(jnp.bfloat16)
        ready = to_high, to_low
        if step:
            near = after(near, to_high).astype(jnp.float32)
            high += near[head:]
            low += after(near[:head], high)
            high = swap_far(collapse(high).astype(jnp.bfloat16), middle)
            outputs.append((collapse(low), high))
        high = own[head:].astype(jnp.float32) + other_high[:head]
        low = own[:head].astype(jnp.float32) + other_low[:head]
        if step + 1 < steps:
            near = swap_near(jnp.concatenate([to_low, to_high]))
    near_high = swap_near(to_high)
    near = swap_near(after(to_low, near_high))
    outputs = [low + after(high, near).astype(jnp.float32) for low, high in outputs]
    high = collapse(high + near_high.astype(jnp.float32))
    low += after(near, high).astype(jnp.float32)
    first = add(low[:tokens], swap_far(high.astype(jnp.bfloat16), middle))
    outputs.append(collapse(jnp.concatenate([first, low[tokens:]])))
    return jnp.stack(outputs).astype(jnp.bfloat16)


def solution(mesh):
    rows = P(None, ("groups", "expert"), None)
    weights = P("expert", None, None)
    return jax.shard_map(
        on_device,
        mesh=mesh,
        in_specs=(rows, rows, rows, P(), weights, weights, weights),
        out_specs=rows,
        check_vma=False,
    )
```

```python
import functools

import jax
import jax.numpy as jnp
from jax import lax
from jax.experimental import pallas as pl
from jax.experimental.pallas import tpu as pltpu
from jax.sharding import PartitionSpec as P

LANES = 128
MIB = 1 << 20


def in_vmem():
    return pl.BlockSpec(memory_space=pltpu.VMEM)


def message_kernel(states_ref, ids_ref, probs_ref, *message_refs):
    steps, tokens, width = states_ref.shape
    tail = message_refs[0].shape[1] - width
    half = tail // 2
    place = lax.broadcasted_iota(jnp.int32, (tail, tokens), 0)
    row = lax.broadcasted_iota(jnp.int32, (tokens, tokens), 0)
    column = lax.broadcasted_iota(jnp.int32, (tokens, tokens), 1)
    one = jnp.where(row == column, 1.0, 0.0).astype(jnp.bfloat16)
    for step in range(steps):
        probs = probs_ref[step]
        share = probs / jnp.sum(probs, axis=0, keepdims=True)
        ids = ids_ref[step]
        dense = jnp.zeros((tail, tokens), jnp.float32)
        for k in range(ids.shape[0]):
            dense += jnp.where(ids[k : k + 1] == place % half, share[k : k + 1], 0.0)
        high = dense.astype(jnp.bfloat16).astype(jnp.float32)
        terms = jnp.where(place < half, high, dense - high).astype(jnp.bfloat16)
        upright = lax.dot_general(one, terms, (((1,), (1,)), ((), ())), preferred_element_type=jnp.float32)
        upright = upright.astype(jnp.bfloat16)
        message_refs[step][:, :width] = states_ref[step]
        message_refs[step][:, width:] = upright


def make_messages(states, ids, probs, tail):
    steps, tokens, width = states.shape
    states, ids, probs = (pltpu.with_memory_space_constraint(x, pltpu.HBM) for x in (states, ids, probs))

    def whole(shape):
        return pl.BlockSpec(shape, lambda i: (0,) * len(shape))

    shapes = [(tokens, width + tail)] * steps
    return pl.pallas_call(
        message_kernel,
        grid=(1,),
        out_shape=[jax.ShapeDtypeStruct(shape, jnp.bfloat16) for shape in shapes],
        in_specs=[whole(x.shape) for x in (states, ids, probs)],
        out_specs=[whole(shape) for shape in shapes],
        compiler_params=pltpu.CompilerParams(vmem_limit_bytes=4 * MIB),
        name="messages",
    )(states, ids, probs)


def load_kernel(*refs):
    count = len(refs) // 3
    copies = [
        pltpu.make_async_copy(refs[i], refs[count + i], refs[2 * count + i]) for i in range(count)
    ]
    for copy in copies:
        copy.start()
    for copy in copies:
        copy.wait()


def load_weights(*arrays):
    arrays = [pltpu.with_memory_space_constraint(x, pltpu.HBM) for x in arrays]
    return pl.pallas_call(
        load_kernel,
        out_shape=[pltpu.VMEM(x.shape, x.dtype) for x in arrays],
        in_specs=[pl.BlockSpec(memory_space=pltpu.HBM)] * len(arrays),
        out_specs=[in_vmem()] * len(arrays),
        scratch_shapes=[pltpu.SemaphoreType.DMA(())] * len(arrays),
        cost_estimate=pl.CostEstimate(flops=0, bytes_accessed=0, transcendentals=0),
        compiler_params=pltpu.CompilerParams(vmem_limit_bytes=4 * MIB),
        name="load_weights",
    )(*arrays)


def expert_kernel(swapped, count, plan, flags_ref, gate_ref, up_ref, down_ref, *refs):
    *sources, own_ref, near_ref, low_ref, high_ref, rows, hidden = refs
    width, units = gate_ref.shape
    tail = rows.shape[1] - width
    owner = lax.axis_index("expert")
    slot = jnp.bitwise_xor(owner, flags_ref[owner]) if swapped else owner
    at = 0
    for source, low, high in plan:
        rows[at : at + high - low] = sources[source][low:high]
        at += high - low
    total = rows.shape[0]
    lane = lax.broadcasted_iota(jnp.int32, (total, tail), 1)
    terms = rows[:, width:].astype(jnp.float32)
    weight = jnp.sum(jnp.where(lane % (tail // 2) == slot, terms, 0.0), axis=1, keepdims=True)
    step = 256
    for at in range(0, units, step):
        gate = jnp.dot(rows[:, :width], gate_ref[:, at : at + step], preferred_element_type=jnp.float32)
        up = jnp.dot(rows[:, :width], up_ref[:, at : at + step], preferred_element_type=jnp.float32)
        value = gate / (1.0 + jnp.exp(-gate)) * up
        hidden[:, at : at + step] = (value * weight).astype(jnp.bfloat16)

    for at in range(0, width, 512):
        part = slice(at, at + 512)
        out = jnp.dot(hidden[...], down_ref[:, part], preferred_element_type=jnp.float32)
        out = out.astype(jnp.bfloat16)
        own_ref[:, part] = out[:count]
        near_ref[:, part] = out[count : 2 * count]
        for side in range(2):
            low, rows_of = (2 + side) * count, slice(side * count // 2, (side + 1) * count // 2)
            low_ref[rows_of, part] = out[low : low + count // 2]
            high_ref[rows_of, part] = out[low + count // 2 : low + count]


def run_expert(swapped, flags, weights, parts, plan):
    total = sum(high - low for _, low, high in plan)
    count = total // 4
    width, units = weights[0].shape
    weights = [pltpu.with_memory_space_constraint(w, pltpu.VMEM) for w in weights]
    return pl.pallas_call(
        functools.partial(expert_kernel, swapped, count, plan),
        out_shape=[jax.ShapeDtypeStruct((count, width), jnp.bfloat16)] * 4,
        in_specs=[pl.BlockSpec(memory_space=pltpu.SMEM)] + [in_vmem()] * (3 + len(parts)),
        out_specs=[in_vmem()] * 4,
        scratch_shapes=[
            pltpu.VMEM((total, parts[0].shape[1]), jnp.bfloat16),
            pltpu.VMEM((total, units), jnp.bfloat16),
        ],
        compiler_params=pltpu.CompilerParams(vmem_limit_bytes=16 * MIB),
        cost_estimate=pl.CostEstimate(
            flops=total * width * units * 6, bytes_accessed=4 * total * width, transcendentals=0
        ),
        name="expert",
    )(flags, *weights, *parts)


def add_kernel(first_ref, second_ref, sum_ref):
    sum_ref[...] = first_ref[...] + second_ref[...].astype(jnp.float32)


def add(first, second):
    return pl.pallas_call(
        add_kernel,
        out_shape=jax.ShapeDtypeStruct(first.shape, jnp.float32),
        in_specs=[in_vmem()] * 2,
        out_specs=in_vmem(),
        compiler_params=pltpu.CompilerParams(vmem_limit_bytes=4 * MIB),
        cost_estimate=pl.CostEstimate(flops=1 << 34, bytes_accessed=0, transcendentals=0),
        name="add",
    )(first, second)


def on_device(states, ids, probs, flags, w_gate, w_up, w_down):
    devices = lax.axis_size("expert")
    lines = devices // 4
    steps, tokens, width = states.shape

    def index(far, near, core):
        return far * 4 + near * 2 + core

    every = [(z, y, c) for z in range(lines) for y in range(2) for c in range(2)]

    def swap_core(x):
        return lax.ppermute(x, "expert", [(index(z, y, c), index(z, y, 1 - c)) for z, y, c in every])

    def swap_near(x):
        return lax.ppermute(x, "expert", [(index(z, y, c), index(z, 1 - y, c)) for z, y, c in every])

    def swap_far(x, by):
        return lax.ppermute(x, "expert", [(index(z, y, c), index(z ^ by, y, c)) for z, y, c in every])

    tail = 2 * devices
    tail = -(-tail // LANES) * LANES
    ids, probs = jnp.swapaxes(ids, 1, 2), jnp.swapaxes(probs, 1, 2)
    middle = lines // 2
    strides = [middle >> shift for shift in range(1, middle.bit_length())]
    head, half = middle * tokens, lines * tokens

    def grow(block, strides):
        for by in strides:
            block = jnp.concatenate([block, swap_far(block, by)])
        return block

    def places(strides):
        found = [0]
        for by in strides:
            found += [place ^ by for place in found]
        return found

    def collapse(block):
        for by in strides[::-1]:
            keep = block.shape[0] // 2
            block = block[:keep] + swap_far(block[keep:].astype(jnp.bfloat16), by).astype(jnp.float32)
        return block

    def after(x, *events):
        return lax.optimization_barrier((x, events))[0]

    w_gate, w_up, w_down = w_gate[0], w_up[0], w_down[0]
    messages = make_messages(states, ids, probs, tail)
    far = swap_far(messages[0], middle)
    close = [messages[0], *[swap_far(messages[0], by) for by in places(strides)[1:]]]
    near_close = [swap_near(messages[0])]
    loaded = load_weights(w_gate, w_up)
    loaded, near_close, close, far = lax.optimization_barrier((loaded, near_close, close, far))
    others = close[1:]
    near_close += [swap_near(block) for block in others]
    crossed = [swap_far(after(message, far), middle) for message in messages[1:]]
    far = grow(far, strides)
    near_far = swap_near(far)
    last = load_weights(after(w_down, far))
    near_own = [swap_near(after(message, others)) for message in messages[1:]]
    crossed, near_close, near_own, last = lax.optimization_barrier((crossed, near_close, near_own, last))
    loaded += last
    line = jnp.concatenate([*close, far, *near_close])
    sources = [[line, swap_core(line), near_far, swap_core(near_far)]]
    wanted = places(strides)
    wanted += [middle ^ place for place in wanted]
    found = places([middle] + strides)
    for message, block, near in zip(messages[1:], crossed, near_own):
        line = grow(jnp.concatenate([message, block]), strides)
        near_line = swap_near(line[tokens:])
        line = jnp.concatenate([line, near])
        sources.append([line, near_line])
    outputs, ready = [], [source[0] for source in sources]
    for step in range(steps):
        plan = []
        for core in range(2):
            if step:
                at = [found.index(place) * tokens for place in wanted]
                plan += [(core, low, low + tokens) for low in at] + [(core, half, half + tokens)]
                plan += [(2 + core, low - tokens, low) for low in at[1:]]
            else:
                plan += [(core, 0, half + head), (2 + core, 0, head)]
        parts = sources[step]
        if step:
            line, near_line = after(sources[step], ready)
            parts = [line, swap_core(line), near_line, swap_core(near_line)]
        own, peer, other_low, other_high = run_expert(step > 0, flags, loaded, after(parts, ready), tuple(plan))
        other_high = swap_core(other_high if step else after(other_high, sources[1][1]))
        if step:
            other_high = after(other_high, near)
        other_high = other_high.astype(jnp.float32)
        other_low = swap_core(after(other_low, near if step else sources[1][1]))
        to_high = (peer[head:].astype(jnp.float32) + other_high[head:]).astype(jnp.bfloat16)
        other_low = after(other_low, to_high).astype(jnp.float32)
        to_low = (peer[:head].astype(jnp.float32) + other_low[head:]).astype(jnp.bfloat16)
        ready = to_high, to_low
        if step:
            near = after(near, to_high).astype(jnp.float32)
            high += near[head:]
            low += after(near[:head], high)
            high = swap_far(collapse(high).astype(jnp.bfloat16), middle)
            outputs.append((collapse(low), high))
        high = own[head:].astype(jnp.float32) + other_high[:head]
        low = own[:head].astype(jnp.float32) + other_low[:head]
        if step + 1 < steps:
            near = swap_near(jnp.concatenate([to_low, to_high]))
    near_high = swap_near(to_high)
    near = swap_near(after(to_low, near_high))
    outputs = [low + after(high, near).astype(jnp.float32) for low, high in outputs]
    high = collapse(high + near_high.astype(jnp.float32))
    low += after(near, high).astype(jnp.float32)
    first = add(low[:tokens], swap_far(high.astype(jnp.bfloat16), middle))
    outputs.append(collapse(jnp.concatenate([first, low[tokens:]])))
    return jnp.stack(outputs).astype(jnp.bfloat16)


def solution(mesh):
    rows = P(None, ("groups", "expert"), None)
    weights = P("expert", None, None)
    return jax.shard_map(
        on_device,
        mesh=mesh,
        in_specs=(rows, rows, rows, P(), weights, weights, weights),
        out_specs=rows,
        check_vma=False,
    )
```
